32 devices in a mesh: grp: 2 (over y), wide: 4 (over z), freq: 2 (over x), pol: 2 (over core).
Axes of the slice: x: 2, y: 2, z: 4, core: 2. Of those that a mesh axis runs over, the one named last changes fastest.
Arguments:
- visibilities: float32 [2, 4096, 8, 384], P(None, ('grp', 'wide'), 'freq', 'pol'), parts along dimension 1, may hold values from -6 to 6
- beams: bfloat16 [8, 8, 2, 384, 768], P('wide', 'freq', None, 'pol'), may hold values from -0.21875 to 0.21875
- spectra: float32 [8, 5, 768], P('freq'), may hold values from 0.1 to 1
- m_orders: int32 [8], replicated, may hold values from 0 to 1023, as said below
Outputs:
- msdata: float32 [16, 8, 2, 384], P(('grp', 'wide'), 'freq', None, 'pol'), parts along dimension 0
- weighted: float32 [16, 8, 2, 384], P(('grp', 'wide'), 'freq', None, 'pol'), parts along dimension 0
The draws below stay inside these ranges and needn't reach their ends.
There are 2 independent parts, one for each index of `grp`. The reference program is written for one: setup_inputs(seed, part) draws one part's arguments, and reference() takes and returns one part's arrays. A program takes and returns all parts, laid end to end along the dimension named above; an argument that names none is the same for every part. Nothing has to cross between parts.
Inputs may be any that keep to these rules, and one draw needn't show every extreme that they name: `m_orders`: the m-orders are distinct, and 0 and 1023 are always among them.
All inputs are finite; a program needn't handle non-finite values.
Results may differ from the reference program's by a relative error of at most 0.0039.
Values sent between devices are 32-bit elements; how exact they have to be, the bound alone decides.
No kernel may reach another device: no remote copies, remote signals or barrier semaphores. Data moves between devices by JAX's collectives and lax.ppermute only.
A program may use at most 64 MiB of HBM per device.

```python
import math
import jax
import jax.numpy as jnp
from jax import lax

TIME = 2048
MODES = 384
DEGREES = 768
BAND = 4
M_TOTAL = 8
FBLOCKS = 8


def draw_m_orders(key, part):
    key_one, key_two = jax.random.split(jax.random.fold_in(key, 11))
    inner = jax.random.permutation(key_one, TIME // 2 - 2)[:M_TOTAL - 2] + 1
    ends = jnp.array([0, TIME // 2 - 1], jnp.int32)
    joined = jnp.concatenate([ends, inner.astype(jnp.int32)])
    return jax.random.permutation(key_two, joined).astype(jnp.int32)


def block_levels(rng, shape, cuts, smallest, high):
    def one(position, parts):
        heights = jax.random.uniform(jax.random.fold_in(jax.random.fold_in(rng, 6), position), (parts,), jnp.float32, smallest / len(cuts), high / len(cuts))
        return jnp.repeat(jnp.exp(heights), shape[position] // parts).reshape((-1,) + (1,) * (len(shape) - position - 1))

    factor_of = one(*cuts[0])
    for cut in cuts[1:]:
        factor_of = factor_of * one(*cut)
    return factor_of


def noise(stream_key, dims, scale, most, pieces=(), kind=jnp.bfloat16):
    values = jax.random.normal(stream_key, dims, jnp.float32) * scale
    if len(pieces) > 0:
        values = block_levels(stream_key, dims, pieces, -0.22, 0.18) * values
    return jnp.clip(values, min=-most, max=most).astype(kind)


def setup_inputs(seed: int = 0, part: int = 0) -> dict:
    key_list = jax.random.split(jax.random.key(seed), 5)
    part_keys = jax.random.split(jax.random.fold_in(key_list[4], part), 5)
    return {
        "visibilities": noise(part_keys[0], (2, TIME, FBLOCKS, MODES), 1.0, 6.0, ((1, 4), (2, 2), (3, 2)), jnp.float32),
        "beams": noise(key_list[1], (M_TOTAL, FBLOCKS, 2, MODES, DEGREES), (2 * MODES) ** -0.5, 0.21875, ((0, 4), (1, 2), (3, 2))),
        "spectra": jnp.clip(jnp.exp(math.log(1.0) - 2.3025851 * jax.random.uniform(key_list[2], (FBLOCKS, BAND + 1, DEGREES), jnp.float32) ** block_levels(key_list[2], (FBLOCKS, BAND + 1, DEGREES), ((0, 2),), -0.2, 0.2)), 0.1, 1.0),
        "m_orders": draw_m_orders(jax.random.fold_in(key_list[4], 71), part),
    }


def fourier_tables(orders, times):
    product = orders[:, None] * times[None, :] % TIME
    angle = product.astype(jnp.float32) * (2.0 * math.pi / TIME)
    factor = 1.0 / math.sqrt(TIME)
    return (jnp.cos(angle) * factor, jnp.sin(angle) * factor)

def reference(visibilities, beams, spectra, m_orders):
    times = jnp.arange(TIME, dtype=jnp.int32)
    cosine, sine_tab = fourier_tables(m_orders.astype(jnp.int32), times)
    data_real = visibilities[0].reshape(TIME, -1)
    data_imag = visibilities[1].reshape(TIME, -1)
    exact_mode = lax.Precision.HIGHEST
    part_real = jnp.dot(cosine, data_real, precision=exact_mode, preferred_element_type=jnp.float32) + jnp.dot(sine_tab, data_imag, precision=exact_mode, preferred_element_type=jnp.float32)
    part_imag = jnp.dot(cosine, data_imag, precision=exact_mode, preferred_element_type=jnp.float32) - jnp.dot(sine_tab, data_real, precision=exact_mode, preferred_element_type=jnp.float32)
    part_real = part_real.reshape(M_TOTAL, FBLOCKS, MODES)
    part_imag = part_imag.reshape(M_TOTAL, FBLOCKS, MODES)
    msdata = jnp.stack([part_real, part_imag], axis=2)

    def per_order(items):
        row_data, beam = items
        rounded = lax.optimization_barrier(row_data.astype(jnp.bfloat16)).astype(jnp.float32)
        beam_full = beam.astype(jnp.float32)
        round_real = rounded[:, 0]
        round_imag = rounded[:, 1]
        stacked = jnp.stack([jnp.stack([round_real, round_imag], 1), jnp.stack([round_imag, -round_real], 1)], 1)
        projected = jnp.einsum('fock,fckl->fol', stacked, beam_full, precision=exact_mode)
        mixed = jnp.zeros(projected.shape, jnp.float32)
        for offset in range(BAND + 1):
            mixed = mixed + spectra[:, offset, None, :] * jnp.roll(projected, -offset, axis=0)
        coupled = lax.optimization_barrier(mixed.astype(jnp.bfloat16)).astype(jnp.float32)
        cop_real = coupled[:, 0]
        cop_imag = coupled[:, 1]
        paired = jnp.stack([jnp.stack([cop_real, -cop_imag], 1), jnp.stack([cop_imag, cop_real], 1)], 1)
        return jnp.einsum('focl,fckl->fok', paired, beam_full, precision=exact_mode)
    weighted = lax.map(per_order, (msdata, beams))
    return (msdata, weighted)
```

```python
import math

import jax
import jax.numpy as jnp
from jax import lax
from jax.experimental import pallas as pl
from jax.experimental.pallas import tpu as pltpu
from jax.sharding import PartitionSpec as P

TIME = 2048
BAND = 4
MIB = 1024 * 1024


def tables(order, time):
    step = (order * time) & (TIME - 1)
    quarter = (step + TIME // 8) >> 9
    x = (step - (quarter << 9)).astype(jnp.float32) * (2.0 * math.pi / TIME)
    y = x * x
    sine = x * (1.0 + y * (-1.0 / 6 + y * (1.0 / 120 + y * (-1.0 / 5040 + y * (1.0 / 362880)))))
    cosine = 1.0 + y * (
        -0.5 + y * (1.0 / 24 + y * (-1.0 / 720 + y * (1.0 / 40320 + y * (-1.0 / 3628800))))
    )
    factor = 1.0 / math.sqrt(TIME)
    odd = (quarter & 1) == 1
    cos_sign = jnp.where(((quarter + 1) & 2) == 2, -factor, factor)
    sin_sign = jnp.where((quarter & 2) == 2, -factor, factor)
    return jnp.where(odd, sine, cosine) * cos_sign, jnp.where(odd, cosine, sine) * sin_sign


def split(value):
    high = value.astype(jnp.bfloat16)
    return high, (value - high.astype(jnp.float32)).astype(jnp.bfloat16)


def dot_last(left, right):
    return lax.dot_general(left, right, (((1,), (1,)), ((), ())), preferred_element_type=jnp.float32)


def transform(visibilities, m_orders, size):
    _, blocks, modes, times = visibilities.shape
    total = m_orders.shape[0]
    per = total // size

    def kernel(orders, vis, *rest):
        outs, (held, sems) = rest[:size], rest[size:]
        copies = [
            [pltpu.make_async_copy(vis.at[c, f], held.at[c, f], sems.at[c, f]) for c in range(2)]
            for f in range(blocks)
        ]
        for pair in copies:
            for copy in pair:
                copy.start()
        me = lax.axis_index("wide")
        row = lax.broadcasted_iota(jnp.int32, (total, times), 0)
        order = jnp.zeros((total, times), jnp.int32)
        for s in range(size):
            for i in range(per):
                order = jnp.where(row == s * per + i, orders[partner(me, s, size) * per + i], order)
        time = lax.broadcasted_iota(jnp.int32, (total, times), 1) + me * times
        cosine, sine = tables(order, time)
        lefts = []
        for c in range(2):
            table = jnp.concatenate([cosine, -sine] if c == 0 else [sine, cosine], 0)
            high, low = split(table)
            lefts.append((jnp.concatenate([high, low], 0), high))
        for f in range(blocks):
            acc = None
            for c in range(2):
                copies[f][c].wait()
                high, low = split(held[c, f])
                both = dot_last(lefts[c][0], high)
                term = both[: 2 * total] + both[2 * total :] + dot_last(lefts[c][1], low)
                acc = term if acc is None else acc + term
            for s in range(size):
                for c in range(2):
                    first = c * total + s * per
                    outs[s][f, c * per : (c + 1) * per, :] = acc[first : first + per]

    return pl.pallas_call(
        kernel,
        out_shape=[jax.ShapeDtypeStruct((blocks, 2 * per, modes), jnp.float32)] * size,
        in_specs=[
            pl.BlockSpec(memory_space=pltpu.SMEM),
            pl.BlockSpec(memory_space=pltpu.HBM),
        ],
        out_specs=[pl.BlockSpec(memory_space=pltpu.VMEM)] * size,
        scratch_shapes=[
            pltpu.VMEM((2, blocks, modes, times), jnp.float32),
            pltpu.SemaphoreType.DMA((2, blocks)),
        ],
        compiler_params=pltpu.CompilerParams(vmem_limit_bytes=12 * MIB),
        name="transform",
    )(m_orders, visibilities)


def project(parts, beams):
    per, blocks, _, modes, degrees = beams.shape
    count = len(parts)

    def kernel(*refs):
        pieces, beam, ms_out, proj_out = refs[:count], refs[count], refs[count + 1], refs[count + 2]
        row = lax.broadcasted_iota(jnp.int32, (2 * per, degrees), 0)
        for f in range(blocks):
            total = pieces[0][f]
            for piece in pieces[1:]:
                total = total + piece[f]
            for r in range(per):
                for c in range(2):
                    ms_out[r, f, c : c + 1, :] = total[c * per + r : c * per + r + 1]
            turned = jnp.concatenate([total[per:], -total[:per]], 0).astype(jnp.bfloat16)
            plain = total.astype(jnp.bfloat16)
            acc = None
            for r in range(per):
                term = jnp.dot(plain, beam[r, f, 0], preferred_element_type=jnp.float32)
                term = term + jnp.dot(turned, beam[r, f, 1], preferred_element_type=jnp.float32)
                acc = term if acc is None else jnp.where(row % per == r, term, acc)
            proj_out[f] = acc

    return pl.pallas_call(
        kernel,
        out_shape=[
            jax.ShapeDtypeStruct((per, blocks, 2, modes), jnp.float32),
            jax.ShapeDtypeStruct((blocks, 2 * per, degrees), jnp.float32),
        ],
        in_specs=[pl.BlockSpec(memory_space=pltpu.VMEM)] * (count + 1),
        out_specs=[pl.BlockSpec(memory_space=pltpu.VMEM)] * 2,
        compiler_params=pltpu.CompilerParams(vmem_limit_bytes=12 * MIB),
        name="project",
    )(*parts, beams)


def couple(own, others, spectra, beams):
    per, blocks, _, modes, degrees = beams.shape

    def kernel(own_ref, pol_ref, next_ref, cross_ref, spec, beam, out):
        row = lax.broadcasted_iota(jnp.int32, (2 * per, modes), 0)
        summed = [own_ref[f] + pol_ref[f] for f in range(blocks)]
        summed += [next_ref[f] + cross_ref[f] for f in range(blocks)]
        for f in range(blocks):
            mixed = None
            for d in range(BAND + 1):
                term = spec[f, d : d + 1, :] * summed[f + d]
                mixed = term if mixed is None else mixed + term
            turned = jnp.concatenate([-mixed[per:], mixed[:per]], 0).astype(jnp.bfloat16)
            plain = mixed.astype(jnp.bfloat16)
            acc = None
            for r in range(per):
                term = dot_last(plain, beam[r, f, 0]) + dot_last(turned, beam[r, f, 1])
                acc = term if acc is None else jnp.where(row % per == r, term, acc)
            for r in range(per):
                for c in range(2):
                    out[r, f, c : c + 1, :] = acc[c * per + r : c * per + r + 1]

    return pl.pallas_call(
        kernel,
        out_shape=jax.ShapeDtypeStruct((per, blocks, 2, modes), jnp.float32),
        in_specs=[pl.BlockSpec(memory_space=pltpu.VMEM)] * 6,
        out_specs=pl.BlockSpec(memory_space=pltpu.VMEM),
        compiler_params=pltpu.CompilerParams(vmem_limit_bytes=12 * MIB),
        name="couple",
    )(own, *others, spectra, beams)


def partner(me, step, size):
    return lax.rem(me + step, size)


def shards(visibilities, beams, spectra, m_orders):
    size = lax.axis_size("wide")
    freqs = lax.axis_size("freq")
    pols = lax.axis_size("pol")
    parts = transform(visibilities.transpose(0, 2, 3, 1), m_orders, size)
    arrived = [parts[0]]
    for s in range(1, size):
        arrived.append(lax.ppermute(parts[s], "wide", [(i, (i + s) % size) for i in range(size)]))
    msdata, partial = project(arrived, beams)

    def fetch(freq_step, pol_step):
        pairs = [
            (((f + freq_step) % freqs) * pols + (p + pol_step) % pols, f * pols + p)
            for f in range(freqs)
            for p in range(pols)
        ]
        return lax.ppermute(partial, ("freq", "pol"), pairs)

    others = [fetch(0, 1), fetch(1, 0), fetch(1, 1)]
    return msdata, couple(partial, others, spectra, beams)


def solution(mesh):
    return jax.shard_map(
        shards,
        mesh=mesh,
        in_specs=(
            P(None, ("grp", "wide"), "freq", "pol"),
            P("wide", "freq", None, "pol", None),
            P("freq", None, None),
            P(),
        ),
        out_specs=(
            P(("grp", "wide"), "freq", None, "pol"),
            P(("grp", "wide"), "freq", None, "pol"),
        ),
        check_vma=False,
    )
```

```python
import math

import jax
import jax.numpy as jnp
from jax import lax
from jax.experimental import pallas as pl
from jax.experimental.pallas import tpu as pltpu
from jax.sharding import PartitionSpec as P

TIME = 2048
BAND = 4
MIB = 1024 * 1024


def tables(order, time):
    step = (order * time) & (TIME - 1)
    quarter = (step + TIME // 8) >> 9
    x = (step - (quarter << 9)).astype(jnp.float32) * (2.0 * math.pi / TIME)
    y = x * x
    sine = x * (1.0 + y * (-1.0 / 6 + y * (1.0 / 120 + y * (-1.0 / 5040 + y * (1.0 / 362880)))))
    cosine = 1.0 + y * (
        -0.5 + y * (1.0 / 24 + y * (-1.0 / 720 + y * (1.0 / 40320 + y * (-1.0 / 3628800))))
    )
    factor = 1.0 / math.sqrt(TIME)
    odd = (quarter & 1) == 1
    cos_sign = jnp.where(((quarter + 1) & 2) == 2, -factor, factor)
    sin_sign = jnp.where((quarter & 2) == 2, -factor, factor)
    return jnp.where(odd, sine, cosine) * cos_sign, jnp.where(odd, cosine, sine) * sin_sign


def split(value):
    high = value.astype(jnp.bfloat16)
    return high, (value - high.astype(jnp.float32)).astype(jnp.bfloat16)


def dot_last(left, right):
    return lax.dot_general(left, right, (((1,), (1,)), ((), ())), preferred_element_type=jnp.float32)


def partner(me, step, size):
    return lax.rem(me + step, size)


def pin(array):
    return pltpu.with_memory_space_constraint(array, pltpu.HBM)


def transform(visibilities, m_orders, size):
    _, points, times = visibilities.shape
    total = m_orders.shape[0]
    per = total // size
    width = 384
    chunks = points // width

    def kernel(orders_ref, vis, *rest):
        out, held, orders, sems, order_sem = rest
        copies = [
            [
                pltpu.make_async_copy(
                    vis.at[c, pl.ds(n * width, width)], held.at[c, n], sems.at[c, n]
                )
                for c in range(2)
            ]
            for n in range(chunks)
        ]
        fetch = pltpu.make_async_copy(orders_ref, orders, order_sem)
        fetch.start()
        for pair in copies:
            for copy in pair:
                copy.start()
        fetch.wait()
        me = lax.axis_index("wide")
        row = lax.broadcasted_iota(jnp.int32, (total, times), 0)
        order = jnp.zeros((total, times), jnp.int32)
        for s in range(size):
            for i in range(per):
                order = jnp.where(row == s * per + i, orders[partner(me, s, size) * per + i], order)
        time = lax.broadcasted_iota(jnp.int32, (total, times), 1) + me * times
        cosine, sine = tables(order, time)
        lefts = []
        for c in range(2):
            table = jnp.concatenate([cosine, -sine] if c == 0 else [sine, cosine], 0)
            high, low = split(table)
            lefts.append((jnp.concatenate([high, low], 0), high))
        for n in range(chunks):
            acc = None
            for c in range(2):
                copies[n][c].wait()
                high, low = split(held[c, n])
                both = dot_last(lefts[c][0], high)
                term = both[: 2 * total] + both[2 * total :] + dot_last(lefts[c][1], low)
                acc = term if acc is None else acc + term
            out[:, pl.ds(n * width, width)] = acc

    return pl.pallas_call(
        kernel,
        out_shape=jax.ShapeDtypeStruct((2 * total, points), jnp.float32),
        in_specs=[pl.BlockSpec(memory_space=pltpu.HBM)] * 2,
        out_specs=pl.BlockSpec(memory_space=pltpu.VMEM),
        scratch_shapes=[
            pltpu.VMEM((2, chunks, width, times), jnp.float32),
            pltpu.SMEM((total,), jnp.int32),
            pltpu.SemaphoreType.DMA((2, chunks)),
            pltpu.SemaphoreType.DMA,
        ],
        compiler_params=pltpu.CompilerParams(vmem_limit_bytes=12 * MIB),
        cost_estimate=pl.CostEstimate(
            flops=4 * 10**9, bytes_accessed=8 * 10**6, transcendentals=0
        ),
        name="transform",
    )(pin(m_orders), pin(visibilities))


def cut(sums, size):
    rows, points = sums.shape
    total = rows // 2
    per = total // size

    def kernel(sums_ref, *outs):
        now = sums_ref[...]
        for s in range(size):
            for c in range(2):
                first = c * total + s * per
                outs[s][c * per : (c + 1) * per, :] = now[first : first + per]

    return pl.pallas_call(
        kernel,
        out_shape=[jax.ShapeDtypeStruct((2 * per, points), jnp.float32)] * size,
        in_specs=[pl.BlockSpec(memory_space=pltpu.VMEM)],
        out_specs=[pl.BlockSpec(memory_space=pltpu.VMEM)] * size,
        compiler_params=pltpu.CompilerParams(vmem_limit_bytes=4 * MIB),
        cost_estimate=pl.CostEstimate(flops=200 * 10**9, bytes_accessed=10**6, transcendentals=0),
        name="cut",
    )(sums)


def project(parts, beams):
    per, blocks, _, modes, degrees = beams.shape
    count = len(parts)

    def kernel(*refs):
        pieces, beam, total_out, proj_out = refs[:count], refs[count], refs[count + 1], refs[count + 2]
        row = lax.broadcasted_iota(jnp.int32, (2 * per, degrees), 0)
        total = pieces[0][...]
        for piece in pieces[1:]:
            total = total + piece[...]
        total_out[...] = total
        plain_all = total.astype(jnp.bfloat16)
        turned_all = jnp.concatenate([total[per:], -total[:per]], 0).astype(jnp.bfloat16)
        for f in range(blocks):
            plain = plain_all[:, f * modes : (f + 1) * modes]
            turned = turned_all[:, f * modes : (f + 1) * modes]
            acc = None
            for r in range(per):
                term = jnp.dot(plain, beam[r, f, 0], preferred_element_type=jnp.float32)
                term = term + jnp.dot(turned, beam[r, f, 1], preferred_element_type=jnp.float32)
                acc = term if acc is None else jnp.where(row % per == r, term, acc)
            proj_out[f] = acc

    return pl.pallas_call(
        kernel,
        out_shape=[
            jax.ShapeDtypeStruct((2 * per, blocks * modes), jnp.float32),
            jax.ShapeDtypeStruct((blocks, 2 * per, degrees), jnp.float32),
        ],
        in_specs=[pl.BlockSpec(memory_space=pltpu.VMEM)] * (count + 1),
        out_specs=[pl.BlockSpec(memory_space=pltpu.VMEM)] * 2,
        compiler_params=pltpu.CompilerParams(vmem_limit_bytes=12 * MIB),
        name="project",
    )(*parts, beams)


def arrange(total, beams):
    per, blocks, _, modes, degrees = beams.shape
    wide = per * modes

    def kernel(total_ref, beam, out, turned):
        total_now = total_ref[...]
        for f in range(blocks):
            block = total_now[:, f * modes : (f + 1) * modes]
            for r in range(per):
                for c in range(2):
                    out[r, f, c : c + 1, :] = block[c * per + r : c * per + r + 1]
            for c in range(2):
                both = jnp.concatenate([beam[r, f, c] for r in range(per)], 0)
                turned[c, :, f * wide : (f + 1) * wide] = both.T

    return pl.pallas_call(
        kernel,
        out_shape=[
            jax.ShapeDtypeStruct((per, blocks, 2, modes), jnp.float32),
            jax.ShapeDtypeStruct((2, degrees, blocks * wide), jnp.bfloat16),
        ],
        in_specs=[pl.BlockSpec(memory_space=pltpu.VMEM)] * 2,
        out_specs=[pl.BlockSpec(memory_space=pltpu.VMEM)] * 2,
        compiler_params=pltpu.CompilerParams(vmem_limit_bytes=16 * MIB),
        name="arrange",
    )(total, beams)


def couple(own, others, spectra, turned_beams, modes):
    blocks, rows, degrees = own.shape
    per = rows // 2
    wide = per * modes

    def kernel(own_ref, cross_ref, next_ref, pol_ref, spec, beam, out):
        summed = [own_ref[f] + pol_ref[f] for f in range(blocks)]
        summed += [next_ref[f] + cross_ref[f] for f in range(blocks)]
        plain, turned = [], []
        for f in range(blocks):
            mixed = None
            for d in range(BAND + 1):
                term = spec[f, d : d + 1, :] * summed[f + d]
                mixed = term if mixed is None else mixed + term
            plain.append(mixed)
            turned.append(jnp.concatenate([-mixed[per:], mixed[:per]], 0))
        plain = jnp.concatenate(plain, 0).astype(jnp.bfloat16)
        turned = jnp.concatenate(turned, 0).astype(jnp.bfloat16)
        acc = jnp.dot(plain, beam[0], preferred_element_type=jnp.float32)
        acc = acc + jnp.dot(turned, beam[1], preferred_element_type=jnp.float32)
        for f in range(blocks):
            for r in range(per):
                first = f * wide + r * modes
                piece = acc[f * rows : (f + 1) * rows, first : first + modes]
                for c in range(2):
                    out[r, f, c : c + 1, :] = piece[c * per + r : c * per + r + 1]

    return pl.pallas_call(
        kernel,
        out_shape=jax.ShapeDtypeStruct((per, blocks, 2, modes), jnp.float32),
        in_specs=[pl.BlockSpec(memory_space=pltpu.VMEM)] * 6,
        out_specs=pl.BlockSpec(memory_space=pltpu.VMEM),
        compiler_params=pltpu.CompilerParams(vmem_limit_bytes=12 * MIB),
        name="couple",
    )(own, *others, spectra, turned_beams)


def shards(visibilities, beams, spectra, m_orders):
    size = lax.axis_size("wide")
    freqs = lax.axis_size("freq")
    pols = lax.axis_size("pol")
    per, blocks, _, modes, _ = beams.shape
    times = visibilities.shape[1]
    sums = transform(
        visibilities.transpose(0, 2, 3, 1).reshape(2, blocks * modes, times), m_orders, size
    )
    parts = cut(sums, size)
    arrived = [parts[0]]
    for s in range(1, size):
        arrived.append(lax.ppermute(parts[s], "wide", [(i, (i + s) % size) for i in range(size)]))
    total, partial = project(arrived, beams)

    def fetch(freq_step, pol_step):
        pairs = [
            (((f + freq_step) % freqs) * pols + (p + pol_step) % pols, f * pols + p)
            for f in range(freqs)
            for p in range(pols)
        ]
        return lax.ppermute(partial, ("freq", "pol"), pairs)

    cross, next_one, pol = fetch(1, 1), fetch(1, 0), fetch(0, 1)
    others = [cross, next_one, pol]
    msdata, turned = arrange(total, beams)
    return msdata, couple(partial, others, spectra, turned, modes)


def solution(mesh):
    return jax.shard_map(
        shards,
        mesh=mesh,
        in_specs=(
            P(None, ("grp", "wide"), "freq", "pol"),
            P("wide", "freq", None, "pol", None),
            P("freq", None, None),
            P(),
        ),
        out_specs=(
            P(("grp", "wide"), "freq", None, "pol"),
            P(("grp", "wide"), "freq", None, "pol"),
        ),
        check_vma=False,
    )
```

```python
import math

import jax
import jax.numpy as jnp
from jax import lax
from jax.experimental import pallas as pl
from jax.experimental.pallas import tpu as pltpu
from jax.sharding import PartitionSpec as P

TIME = 2048
BAND = 4
MIB = 1024 * 1024
PLAN = ((1, 3, 2, 0), (2, 1, 0, 3), (3, 0, 2, 1), (0, 2, 1, 3), (0, 1, 3, 2))


def tables(order, time):
    step = (order * time) & (TIME - 1)
    quarter = (step + TIME // 8) >> 9
    x = (step - (quarter << 9)).astype(jnp.float32) * (2.0 * math.pi / TIME)
    y = x * x
    sine = x * (1.0 + y * (-1.0 / 6 + y * (1.0 / 120 + y * (-1.0 / 5040 + y * (1.0 / 362880)))))
    cosine = 1.0 + y * (
        -0.5 + y * (1.0 / 24 + y * (-1.0 / 720 + y * (1.0 / 40320 + y * (-1.0 / 3628800))))
    )
    factor = 1.0 / math.sqrt(TIME)
    odd = (quarter & 1) == 1
    cos_sign = jnp.where(((quarter + 1) & 2) == 2, -factor, factor)
    sin_sign = jnp.where((quarter & 2) == 2, -factor, factor)
    return jnp.where(odd, sine, cosine) * cos_sign, jnp.where(odd, cosine, sine) * sin_sign


def split(value):
    high = value.astype(jnp.bfloat16)
    return high, (value - high.astype(jnp.float32)).astype(jnp.bfloat16)


def dot_last(left, right):
    return lax.dot_general(left, right, (((1,), (1,)), ((), ())), preferred_element_type=jnp.float32)


def pairs_of(step, pols):
    return [
        (w * pols + p, to * pols + (p if to != w else (p + 1) % pols))
        for w, to in enumerate(step)
        for p in range(pols)
    ]


def pin(array):
    return pltpu.with_memory_space_constraint(array, pltpu.HBM)


def transform(visibilities, m_orders, size):
    _, points, times = visibilities.shape
    total = m_orders.shape[0]
    per = total // size
    width = 384
    chunks = points // width

    def kernel(orders_ref, vis, *rest):
        out, held, orders, sems, order_sem = rest
        copies = [
            [
                pltpu.make_async_copy(
                    vis.at[c, pl.ds(n * width, width)], held.at[c, n], sems.at[c, n]
                )
                for c in range(2)
            ]
            for n in range(chunks)
        ]
        fetch = pltpu.make_async_copy(orders_ref, orders, order_sem)
        fetch.start()
        for pair in copies:
            for copy in pair:
                copy.start()
        fetch.wait()
        me = lax.axis_index("wide")
        row = lax.broadcasted_iota(jnp.int32, (total, times), 0)
        order = jnp.zeros((total, times), jnp.int32)
        for i in range(total):
            order = jnp.where(row == i, orders[i], order)
        time = lax.broadcasted_iota(jnp.int32, (total, times), 1) + me * times
        cosine, sine = tables(order, time)
        lefts = []
        for c in range(2):
            table = jnp.concatenate([cosine, -sine] if c == 0 else [sine, cosine], 0)
            high, low = split(table)
            lefts.append(jnp.concatenate([high, low], 0))
        for n in range(chunks):
            for copy in copies[n]:
                copy.wait()
            acc = None
            for c in range(2):
                high, low = split(held[c, n])
                both = dot_last(lefts[c], jnp.concatenate([high, low], 0))
                term = both[: 2 * total, :width] + both[2 * total :, :width] + both[: 2 * total, width:]
                acc = term if acc is None else acc + term
            for s in range(size):
                for c in range(2):
                    first = c * total + s * per
                    out[s, c * per : (c + 1) * per, pl.ds(n * width, width)] = acc[first : first + per]

    return pl.pallas_call(
        kernel,
        out_shape=jax.ShapeDtypeStruct((size, 2 * per, points), jnp.float32),
        in_specs=[pl.BlockSpec(memory_space=pltpu.HBM)] * 2,
        out_specs=pl.BlockSpec(memory_space=pltpu.VMEM),
        scratch_shapes=[
            pltpu.VMEM((2, chunks, width, times), jnp.float32),
            pltpu.SMEM((total,), jnp.int32),
            pltpu.SemaphoreType.DMA((2, chunks)),
            pltpu.SemaphoreType.DMA,
        ],
        compiler_params=pltpu.CompilerParams(vmem_limit_bytes=12 * MIB),
        cost_estimate=pl.CostEstimate(
            flops=4 * 10**9, bytes_accessed=8 * 10**6, transcendentals=0
        ),
        name="transform",
    )(pin(m_orders), pin(visibilities))


def cut(sums, plan):
    size, rows, points = sums.shape

    def kernel(sums_ref, *outs):
        me = lax.axis_index("wide")
        outs[0][...] = sums_ref[me]
        for out, step in zip(outs[1:], plan):
            to = jnp.int32(step[0])
            for w in range(1, size):
                to = jnp.where(me == w, step[w], to)
            if any(step[w] == w for w in range(size)):
                out[...] = jnp.where(to == me, 0.0, sums_ref[to])
            else:
                out[...] = sums_ref[to]

    return pl.pallas_call(
        kernel,
        out_shape=[jax.ShapeDtypeStruct((rows, points), jnp.float32)] * (len(plan) + 1),
        in_specs=[pl.BlockSpec(memory_space=pltpu.VMEM)],
        out_specs=[pl.BlockSpec(memory_space=pltpu.VMEM)] * (len(plan) + 1),
        compiler_params=pltpu.CompilerParams(vmem_limit_bytes=4 * MIB),
        cost_estimate=pl.CostEstimate(flops=200 * 10**9, bytes_accessed=10**6, transcendentals=0),
        name="cut",
    )(sums)


def project(parts, beams):
    per, blocks, _, modes, degrees = beams.shape
    count = len(parts)

    def kernel(*refs):
        pieces, beam, total_out, proj_out = refs[:count], refs[count], refs[count + 1], refs[count + 2]
        row = lax.broadcasted_iota(jnp.int32, (2 * per, degrees), 0)
        total = pieces[0][...]
        for piece in pieces[1:]:
            total = total + piece[...]
        total_out[...] = total
        plain_all = total.astype(jnp.bfloat16)
        turned_all = jnp.concatenate([total[per:], -total[:per]], 0).astype(jnp.bfloat16)
        for f in range(blocks):
            plain = plain_all[:, f * modes : (f + 1) * modes]
            turned = turned_all[:, f * modes : (f + 1) * modes]
            acc = None
            for r in range(per):
                term = jnp.dot(plain, beam[r, f, 0], preferred_element_type=jnp.float32)
                term = term + jnp.dot(turned, beam[r, f, 1], preferred_element_type=jnp.float32)
                acc = term if acc is None else jnp.where(row % per == r, term, acc)
            proj_out[f] = acc

    return pl.pallas_call(
        kernel,
        out_shape=[
            jax.ShapeDtypeStruct((2 * per, blocks * modes), jnp.float32),
            jax.ShapeDtypeStruct((blocks, 2 * per, degrees), jnp.float32),
        ],
        in_specs=[pl.BlockSpec(memory_space=pltpu.VMEM)] * (count + 1),
        out_specs=[pl.BlockSpec(memory_space=pltpu.VMEM)] * 2,
        compiler_params=pltpu.CompilerParams(vmem_limit_bytes=12 * MIB),
        name="project",
    )(*parts, beams)


def arrange(total, beams):
    per, blocks, _, modes, degrees = beams.shape
    wide = per * modes

    def kernel(total_ref, beam, out, turned):
        total_now = total_ref[...]
        for f in range(blocks):
            block = total_now[:, f * modes : (f + 1) * modes]
            for r in range(per):
                for c in range(2):
                    out[r, f, c : c + 1, :] = block[c * per + r : c * per + r + 1]
            for c in range(2):
                both = jnp.concatenate([beam[r, f, c] for r in range(per)], 0)
                turned[c, :, f * wide : (f + 1) * wide] = both.T

    return pl.pallas_call(
        kernel,
        out_shape=[
            jax.ShapeDtypeStruct((per, blocks, 2, modes), jnp.float32),
            jax.ShapeDtypeStruct((2, degrees, blocks * wide), jnp.bfloat16),
        ],
        in_specs=[pl.BlockSpec(memory_space=pltpu.VMEM)] * 2,
        out_specs=[pl.BlockSpec(memory_space=pltpu.VMEM)] * 2,
        compiler_params=pltpu.CompilerParams(vmem_limit_bytes=16 * MIB),
        name="arrange",
    )(total, beams)


def couple(own, following, spectra, turned_beams, modes):
    blocks, rows, degrees = own.shape
    per = rows // 2
    wide = per * modes

    def kernel(own_ref, next_ref, spec, beam, out):
        summed = [own_ref[f] for f in range(blocks)] + [next_ref[f] for f in range(blocks)]
        plain, turned = [], []
        for f in range(blocks):
            mixed = None
            for d in range(BAND + 1):
                term = spec[f, d : d + 1, :] * summed[f + d]
                mixed = term if mixed is None else mixed + term
            plain.append(mixed)
            turned.append(jnp.concatenate([-mixed[per:], mixed[:per]], 0))
        plain = jnp.concatenate(plain, 0).astype(jnp.bfloat16)
        turned = jnp.concatenate(turned, 0).astype(jnp.bfloat16)
        acc = jnp.dot(plain, beam[0], preferred_element_type=jnp.float32)
        acc = acc + jnp.dot(turned, beam[1], preferred_element_type=jnp.float32)
        for f in range(blocks):
            for r in range(per):
                first = f * wide + r * modes
                piece = acc[f * rows : (f + 1) * rows, first : first + modes]
                for c in range(2):
                    out[r, f, c : c + 1, :] = piece[c * per + r : c * per + r + 1]

    return pl.pallas_call(
        kernel,
        out_shape=jax.ShapeDtypeStruct((per, blocks, 2, modes), jnp.float32),
        in_specs=[pl.BlockSpec(memory_space=pltpu.VMEM)] * 4,
        out_specs=pl.BlockSpec(memory_space=pltpu.VMEM),
        compiler_params=pltpu.CompilerParams(vmem_limit_bytes=12 * MIB),
        name="couple",
    )(own, following, spectra, turned_beams)


def shards(visibilities, beams, spectra, m_orders):
    size = lax.axis_size("wide")
    freqs = lax.axis_size("freq")
    pols = lax.axis_size("pol")
    per, blocks, _, modes, _ = beams.shape
    times = visibilities.shape[1]
    sums = transform(
        visibilities.transpose(0, 2, 3, 1).reshape(2, blocks * modes, times), m_orders, size
    )
    plan = PLAN if size == 4 else [[(w + s) % size for w in range(size)] for s in range(1, size)]
    own, *parts = cut(sums, plan)
    arrived = [own] + [
        lax.ppermute(part, ("wide", "pol"), pairs_of(step, pols)) for part, step in zip(parts, plan)
    ]
    total, partial = project(arrived, beams)

    other = lax.ppermute(partial, "pol", [(p, (p + 1) % pols) for p in range(pols)])
    projected = partial + other
    pairs = [
        (((f + 1) % freqs) * pols + (p + 1) % pols, f * pols + p)
        for f in range(freqs)
        for p in range(pols)
    ]
    following = lax.ppermute(projected, ("freq", "pol"), pairs)
    msdata, turned = arrange(total, beams)
    return msdata, couple(projected, following, spectra, turned, modes)


def solution(mesh):
    return jax.shard_map(
        shards,
        mesh=mesh,
        in_specs=(
            P(None, ("grp", "wide"), "freq", "pol"),
            P("wide", "freq", None, "pol", None),
            P("freq", None, None),
            P(),
        ),
        out_specs=(
            P(("grp", "wide"), "freq", None, "pol"),
            P(("grp", "wide"), "freq", None, "pol"),
        ),
        check_vma=False,
    )
```

```python
import math

import jax
import jax.numpy as jnp
from jax import lax
from jax.experimental import pallas as pl
from jax.experimental.pallas import tpu as pltpu
from jax.sharding import PartitionSpec as P

TIME = 2048
BAND = 4
MIB = 1024 * 1024
PLAN = ((1, 3, 2, 0), (2, 1, 0, 3), (3, 0, 2, 1), (0, 2, 1, 3), (0, 1, 3, 2))


def tables(order, time):
    step = (order * time) & (TIME - 1)
    quarter = (step + TIME // 8) >> 9
    x = (step - (quarter << 9)).astype(jnp.float32) * (2.0 * math.pi / TIME)
    y = x * x
    sine = x * (1.0 + y * (-1.0 / 6 + y * (1.0 / 120 + y * (-1.0 / 5040 + y * (1.0 / 362880)))))
    cosine = 1.0 + y * (
        -0.5 + y * (1.0 / 24 + y * (-1.0 / 720 + y * (1.0 / 40320 + y * (-1.0 / 3628800))))
    )
    factor = 1.0 / math.sqrt(TIME)
    odd = (quarter & 1) == 1
    cos_sign = jnp.where(((quarter + 1) & 2) == 2, -factor, factor)
    sin_sign = jnp.where((quarter & 2) == 2, -factor, factor)
    return jnp.where(odd, sine, cosine) * cos_sign, jnp.where(odd, cosine, sine) * sin_sign


def split(value):
    high = value.astype(jnp.bfloat16)
    return high, (value - high.astype(jnp.float32)).astype(jnp.bfloat16)


def dot_last(left, right):
    return lax.dot_general(left, right, (((1,), (1,)), ((), ())), preferred_element_type=jnp.float32)


def pairs_of(step, pols):
    return [
        (w * pols + p, to * pols + (p if to != w else (p + 1) % pols))
        for w, to in enumerate(step)
        for p in range(pols)
    ]


def pin(array):
    return pltpu.with_memory_space_constraint(array, pltpu.HBM)


def transform(visibilities, m_orders, size):
    _, points, times = visibilities.shape
    total = m_orders.shape[0]
    per = total // size
    width = 256
    chunks = points // width

    def kernel(orders_ref, vis, *rest):
        out, held, orders, sems, order_sem = rest
        copies = [
            [
                pltpu.make_async_copy(
                    vis.at[c, pl.ds(n * width, width)], held.at[c, n], sems.at[c, n]
                )
                for c in range(2)
            ]
            for n in range(chunks)
        ]
        fetch = pltpu.make_async_copy(orders_ref, orders, order_sem)
        fetch.start()
        for pair in copies:
            for copy in pair:
                copy.start()
        fetch.wait()
        me = lax.axis_index("wide")
        row = lax.broadcasted_iota(jnp.int32, (total, times), 0)
        order = jnp.zeros((total, times), jnp.int32)
        for i in range(total):
            order = jnp.where(row == i, orders[i], order)
        time = lax.broadcasted_iota(jnp.int32, (total, times), 1) + me * times
        cosine, sine = tables(order, time)
        lefts = []
        for c in range(2):
            table = jnp.concatenate([cosine, -sine] if c == 0 else [sine, cosine], 0)
            high, low = split(table)
            lefts.append(jnp.concatenate([high, low], 0))
        for n in range(chunks):
            for copy in copies[n]:
                copy.wait()
            acc, small = None, None
            for c in range(2):
                high, low = split(held[c, n])
                rest = dot_last(low, lefts[c][: 2 * total])
                small = rest if small is None else small + rest
                both = dot_last(lefts[c], high)
                term = both[: 2 * total] + both[2 * total :]
                acc = term if acc is None else acc + term
            acc = acc + small.T
            for s in range(size):
                for c in range(2):
                    first = c * total + s * per
                    out[s, c * per : (c + 1) * per, pl.ds(n * width, width)] = acc[first : first + per]

    return pl.pallas_call(
        kernel,
        out_shape=jax.ShapeDtypeStruct((size, 2 * per, points), jnp.float32),
        in_specs=[pl.BlockSpec(memory_space=pltpu.HBM)] * 2,
        out_specs=pl.BlockSpec(memory_space=pltpu.VMEM),
        scratch_shapes=[
            pltpu.VMEM((2, chunks, width, times), jnp.float32),
            pltpu.SMEM((total,), jnp.int32),
            pltpu.SemaphoreType.DMA((2, chunks)),
            pltpu.SemaphoreType.DMA,
        ],
        compiler_params=pltpu.CompilerParams(vmem_limit_bytes=12 * MIB),
        cost_estimate=pl.CostEstimate(
            flops=4 * 10**9, bytes_accessed=8 * 10**6, transcendentals=0
        ),
        name="transform",
    )(pin(m_orders), pin(visibilities))


def cut(sums, plan):
    size, rows, points = sums.shape

    def kernel(sums_ref, *outs):
        me = lax.axis_index("wide")
        outs[0][...] = sums_ref[me]
        for out, step in zip(outs[1:], plan):
            to = jnp.int32(step[0])
            for w in range(1, size):
                to = jnp.where(me == w, step[w], to)
            if any(step[w] == w for w in range(size)):
                out[...] = jnp.where(to == me, 0.0, sums_ref[to])
            else:
                out[...] = sums_ref[to]

    return pl.pallas_call(
        kernel,
        out_shape=[jax.ShapeDtypeStruct((rows, points), jnp.float32)] * (len(plan) + 1),
        in_specs=[pl.BlockSpec(memory_space=pltpu.VMEM)],
        out_specs=[pl.BlockSpec(memory_space=pltpu.VMEM)] * (len(plan) + 1),
        compiler_params=pltpu.CompilerParams(vmem_limit_bytes=4 * MIB),
        cost_estimate=pl.CostEstimate(flops=200 * 10**9, bytes_accessed=10**6, transcendentals=0),
        name="cut",
    )(sums)


def project(parts, beams):
    per, blocks, _, modes, degrees = beams.shape
    count = len(parts)

    def kernel(*refs):
        pieces, beam, total_out, proj_out = refs[:count], refs[count], refs[count + 1], refs[count + 2]
        row = lax.broadcasted_iota(jnp.int32, (2 * per, degrees), 0)
        total = pieces[0][...]
        for piece in pieces[1:]:
            total = total + piece[...]
        total_out[...] = total
        plain_all = total.astype(jnp.bfloat16)
        turned_all = jnp.concatenate([total[per:], -total[:per]], 0).astype(jnp.bfloat16)
        for f in range(blocks):
            plain = plain_all[:, f * modes : (f + 1) * modes]
            turned = turned_all[:, f * modes : (f + 1) * modes]
            acc = None
            for r in range(per):
                term = jnp.dot(plain, beam[r, f, 0], preferred_element_type=jnp.float32)
                term = term + jnp.dot(turned, beam[r, f, 1], preferred_element_type=jnp.float32)
                acc = term if acc is None else jnp.where(row % per == r, term, acc)
            proj_out[f] = acc

    return pl.pallas_call(
        kernel,
        out_shape=[
            jax.ShapeDtypeStruct((2 * per, blocks * modes), jnp.float32),
            jax.ShapeDtypeStruct((blocks, 2 * per, degrees), jnp.float32),
        ],
        in_specs=[pl.BlockSpec(memory_space=pltpu.VMEM)] * (count + 1),
        out_specs=[pl.BlockSpec(memory_space=pltpu.VMEM)] * 2,
        compiler_params=pltpu.CompilerParams(vmem_limit_bytes=12 * MIB),
        name="project",
    )(*parts, beams)


def arrange(total, beams):
    per, blocks, _, modes, degrees = beams.shape
    wide = per * modes

    def kernel(total_ref, beam, out, turned):
        total_now = total_ref[...]
        for f in range(blocks):
            block = total_now[:, f * modes : (f + 1) * modes]
            for r in range(per):
                for c in range(2):
                    out[r, f, c : c + 1, :] = block[c * per + r : c * per + r + 1]
            for c in range(2):
                both = jnp.concatenate([beam[r, f, c] for r in range(per)], 0)
                turned[c, :, f * wide : (f + 1) * wide] = both.T

    return pl.pallas_call(
        kernel,
        out_shape=[
            jax.ShapeDtypeStruct((per, blocks, 2, modes), jnp.float32),
            jax.ShapeDtypeStruct((2, degrees, blocks * wide), jnp.bfloat16),
        ],
        in_specs=[pl.BlockSpec(memory_space=pltpu.VMEM)] * 2,
        out_specs=[pl.BlockSpec(memory_space=pltpu.VMEM)] * 2,
        compiler_params=pltpu.CompilerParams(vmem_limit_bytes=16 * MIB),
        name="arrange",
    )(total, beams)


def couple(own, others, spectra, turned_beams, modes):
    blocks, rows, degrees = own.shape
    per = rows // 2
    wide = per * modes

    def kernel(own_ref, cross_ref, next_ref, pol_ref, spec, beam, out):
        summed = [own_ref[f] + pol_ref[f] for f in range(blocks)]
        summed += [next_ref[f] + cross_ref[f] for f in range(blocks)]
        plain, turned = [], []
        for f in range(blocks):
            mixed = None
            for d in range(BAND + 1):
                term = spec[f, d : d + 1, :] * summed[f + d]
                mixed = term if mixed is None else mixed + term
            plain.append(mixed)
            turned.append(jnp.concatenate([-mixed[per:], mixed[:per]], 0))
        plain = jnp.concatenate(plain, 0).astype(jnp.bfloat16)
        turned = jnp.concatenate(turned, 0).astype(jnp.bfloat16)
        acc = jnp.dot(plain, beam[0], preferred_element_type=jnp.float32)
        acc = acc + jnp.dot(turned, beam[1], preferred_element_type=jnp.float32)
        for f in range(blocks):
            for r in range(per):
                first = f * wide + r * modes
                piece = acc[f * rows : (f + 1) * rows, first : first + modes]
                for c in range(2):
                    out[r, f, c : c + 1, :] = piece[c * per + r : c * per + r + 1]

    return pl.pallas_call(
        kernel,
        out_shape=jax.ShapeDtypeStruct((per, blocks, 2, modes), jnp.float32),
        in_specs=[pl.BlockSpec(memory_space=pltpu.VMEM)] * 6,
        out_specs=pl.BlockSpec(memory_space=pltpu.VMEM),
        compiler_params=pltpu.CompilerParams(vmem_limit_bytes=12 * MIB),
        name="couple",
    )(own, *others, spectra, turned_beams)


def shards(visibilities, beams, spectra, m_orders):
    size = lax.axis_size("wide")
    freqs = lax.axis_size("freq")
    pols = lax.axis_size("pol")
    per, blocks, _, modes, _ = beams.shape
    times = visibilities.shape[1]
    sums = transform(
        visibilities.transpose(0, 2, 3, 1).reshape(2, blocks * modes, times), m_orders, size
    )
    plan = PLAN if size == 4 else [[(w + s) % size for w in range(size)] for s in range(1, size)]
    own, *parts = cut(sums, plan)
    arrived = [own] + [
        lax.ppermute(part, ("wide", "pol"), pairs_of(step, pols)) for part, step in zip(parts, plan)
    ]
    total, partial = project(arrived, beams)

    def fetch(freq_step, pol_step):
        pairs = [
            (((f + freq_step) % freqs) * pols + (p + pol_step) % pols, f * pols + p)
            for f in range(freqs)
            for p in range(pols)
        ]
        return lax.ppermute(partial, ("freq", "pol"), pairs)

    cross, following, pol = fetch(1, 1), fetch(1, 0), fetch(0, 1)
    others = [cross, following, pol]
    msdata, turned = arrange(total, beams)
    return msdata, couple(partial, others, spectra, turned, modes)


def solution(mesh):
    return jax.shard_map(
        shards,
        mesh=mesh,
        in_specs=(
            P(None, ("grp", "wide"), "freq", "pol"),
            P("wide", "freq", None, "pol", None),
            P("freq", None, None),
            P(),
        ),
        out_specs=(
            P(("grp", "wide"), "freq", None, "pol"),
            P(("grp", "wide"), "freq", None, "pol"),
        ),
        check_vma=False,
    )
```

```python
import math

import jax
import jax.numpy as jnp
from jax import lax
from jax.experimental import pallas as pl
from jax.experimental.pallas import tpu as pltpu
from jax.sharding import PartitionSpec as P

TIME = 2048
BAND = 4
MIB = 1024 * 1024
PLAN = ((1, 3, 2, 0), (2, 1, 0, 3), (3, 0, 2, 1), (0, 2, 1, 3), (0, 1, 3, 2))


def tables(order, time):
    step = (order * time) & (TIME - 1)
    quarter = (step + TIME // 8) >> 9
    x = (step - (quarter << 9)).astype(jnp.float32) * (2.0 * math.pi / TIME)
    y = x * x
    sine = x * (1.0 + y * (-1.0 / 6 + y * (1.0 / 120 + y * (-1.0 / 5040 + y * (1.0 / 362880)))))
    cosine = 1.0 + y * (
        -0.5 + y * (1.0 / 24 + y * (-1.0 / 720 + y * (1.0 / 40320 + y * (-1.0 / 3628800))))
    )
    factor = 1.0 / math.sqrt(TIME)
    odd = (quarter & 1) == 1
    cos_sign = jnp.where(((quarter + 1) & 2) == 2, -factor, factor)
    sin_sign = jnp.where((quarter & 2) == 2, -factor, factor)
    return jnp.where(odd, sine, cosine) * cos_sign, jnp.where(odd, cosine, sine) * sin_sign


def split(value):
    high = value.astype(jnp.bfloat16)
    return high, (value - high.astype(jnp.float32)).astype(jnp.bfloat16)


def dot_last(left, right):
    return lax.dot_general(left, right, (((1,), (1,)), ((), ())), preferred_element_type=jnp.float32)


def pairs_of(step, pols):
    return [
        (w * pols + p, to * pols + (p if to != w else (p + 1) % pols))
        for w, to in enumerate(step)
        for p in range(pols)
    ]


def pin(array):
    return pltpu.with_memory_space_constraint(array, pltpu.HBM)


def transform(visibilities, m_orders, size):
    _, points, times = visibilities.shape
    total = m_orders.shape[0]
    per = total // size
    width = 256
    chunks = points // width

    def kernel(orders_ref, vis, *rest):
        out, held, orders, sems, order_sem = rest
        copies = [
            [
                pltpu.make_async_copy(
                    vis.at[c, pl.ds(n * width, width)], held.at[c, n], sems.at[c, n]
                )
                for c in range(2)
            ]
            for n in range(chunks)
        ]
        fetch = pltpu.make_async_copy(orders_ref, orders, order_sem)
        fetch.start()
        for pair in copies:
            for copy in pair:
                copy.start()
        fetch.wait()
        me = lax.axis_index("wide")
        row = lax.broadcasted_iota(jnp.int32, (total, times), 0)
        order = jnp.zeros((total, times), jnp.int32)
        for i in range(total):
            order = jnp.where(row == i, orders[i], order)
        time = lax.broadcasted_iota(jnp.int32, (total, times), 1) + me * times
        cosine, sine = tables(order, time)
        lefts = []
        for c in range(2):
            table = jnp.concatenate([cosine, -sine] if c == 0 else [sine, cosine], 0)
            high, low = split(table)
            lefts.append(jnp.concatenate([high, low], 0))
        sums = []
        for n in range(chunks):
            for copy in copies[n]:
                copy.wait()
            acc, small = None, None
            for c in range(2):
                high, low = split(held[c, n])
                rest = dot_last(low, lefts[c][: 2 * total])
                small = rest if small is None else small + rest
                both = dot_last(lefts[c], high)
                term = both[: 2 * total] + both[2 * total :]
                acc = term if acc is None else acc + term
            sums.append((acc, small))
        for n in range(chunks):
            acc = sums[n][0] + sums[n][1].T
            for s in range(size):
                for c in range(2):
                    first = c * total + s * per
                    out[s, c * per : (c + 1) * per, pl.ds(n * width, width)] = acc[first : first + per]

    return pl.pallas_call(
        kernel,
        out_shape=jax.ShapeDtypeStruct((size, 2 * per, points), jnp.float32),
        in_specs=[pl.BlockSpec(memory_space=pltpu.HBM)] * 2,
        out_specs=pl.BlockSpec(memory_space=pltpu.VMEM),
        scratch_shapes=[
            pltpu.VMEM((2, chunks, width, times), jnp.float32),
            pltpu.SMEM((total,), jnp.int32),
            pltpu.SemaphoreType.DMA((2, chunks)),
            pltpu.SemaphoreType.DMA,
        ],
        compiler_params=pltpu.CompilerParams(vmem_limit_bytes=12 * MIB),
        cost_estimate=pl.CostEstimate(
            flops=4 * 10**9, bytes_accessed=8 * 10**6, transcendentals=0
        ),
        name="transform",
    )(pin(m_orders), pin(visibilities))


def cut(sums, plan):
    size, rows, points = sums.shape

    def kernel(sums_ref, *outs):
        me = lax.axis_index("wide")
        outs[0][...] = sums_ref[me]
        for out, step in zip(outs[1:], plan):
            to = jnp.int32(step[0])
            for w in range(1, size):
                to = jnp.where(me == w, step[w], to)
            if any(step[w] == w for w in range(size)):
                out[...] = jnp.where(to == me, 0.0, sums_ref[to])
            else:
                out[...] = sums_ref[to]

    return pl.pallas_call(
        kernel,
        out_shape=[jax.ShapeDtypeStruct((rows, points), jnp.float32)] * (len(plan) + 1),
        in_specs=[pl.BlockSpec(memory_space=pltpu.VMEM)],
        out_specs=[pl.BlockSpec(memory_space=pltpu.VMEM)] * (len(plan) + 1),
        compiler_params=pltpu.CompilerParams(vmem_limit_bytes=4 * MIB),
        cost_estimate=pl.CostEstimate(flops=200 * 10**9, bytes_accessed=10**6, transcendentals=0),
        name="cut",
    )(sums)


def project(parts, beams):
    per, blocks, _, modes, degrees = beams.shape
    count = len(parts)

    def kernel(*refs):
        pieces, beam, total_out, proj_out = refs[:count], refs[count], refs[count + 1], refs[count + 2]
        row = lax.broadcasted_iota(jnp.int32, (2 * per, degrees), 0)
        total = pieces[0][...]
        for piece in pieces[1:]:
            total = total + piece[...]
        total_out[...] = total
        plain_all = total.astype(jnp.bfloat16)
        turned_all = jnp.concatenate([total[per:], -total[:per]], 0).astype(jnp.bfloat16)
        for f in range(blocks):
            plain = plain_all[:, f * modes : (f + 1) * modes]
            turned = turned_all[:, f * modes : (f + 1) * modes]
            acc = None
            for r in range(per):
                term = jnp.dot(plain, beam[r, f, 0], preferred_element_type=jnp.float32)
                term = term + jnp.dot(turned, beam[r, f, 1], preferred_element_type=jnp.float32)
                acc = term if acc is None else jnp.where(row % per == r, term, acc)
            proj_out[f] = acc

    return pl.pallas_call(
        kernel,
        out_shape=[
            jax.ShapeDtypeStruct((2 * per, blocks * modes), jnp.float32),
            jax.ShapeDtypeStruct((blocks, 2 * per, degrees), jnp.float32),
        ],
        in_specs=[pl.BlockSpec(memory_space=pltpu.VMEM)] * (count + 1),
        out_specs=[pl.BlockSpec(memory_space=pltpu.VMEM)] * 2,
        compiler_params=pltpu.CompilerParams(vmem_limit_bytes=12 * MIB),
        name="project",
    )(*parts, beams)


def arrange(total, beams):
    per, blocks, _, modes, degrees = beams.shape
    wide = per * modes

    def kernel(total_ref, beam, out, turned):
        total_now = total_ref[...]
        for f in range(blocks):
            block = total_now[:, f * modes : (f + 1) * modes]
            for r in range(per):
                for c in range(2):
                    out[r, f, c : c + 1, :] = block[c * per + r : c * per + r + 1]
            for c in range(2):
                both = jnp.concatenate([beam[r, f, c] for r in range(per)], 0)
                turned[c, :, f * wide : (f + 1) * wide] = both.T

    return pl.pallas_call(
        kernel,
        out_shape=[
            jax.ShapeDtypeStruct((per, blocks, 2, modes), jnp.float32),
            jax.ShapeDtypeStruct((2, degrees, blocks * wide), jnp.bfloat16),
        ],
        in_specs=[pl.BlockSpec(memory_space=pltpu.VMEM)] * 2,
        out_specs=[pl.BlockSpec(memory_space=pltpu.VMEM)] * 2,
        compiler_params=pltpu.CompilerParams(vmem_limit_bytes=16 * MIB),
        name="arrange",
    )(total, beams)


def couple(own, others, spectra, turned_beams, modes):
    blocks, rows, degrees = own.shape
    per = rows // 2
    wide = per * modes

    def kernel(own_ref, cross_ref, next_ref, pol_ref, spec, beam, out):
        summed = [own_ref[f] + pol_ref[f] for f in range(blocks)]
        summed += [next_ref[f] + cross_ref[f] for f in range(blocks)]
        plain, turned = [], []
        for f in range(blocks):
            mixed = None
            for d in range(BAND + 1):
                term = spec[f, d : d + 1, :] * summed[f + d]
                mixed = term if mixed is None else mixed + term
            plain.append(mixed)
            turned.append(jnp.concatenate([-mixed[per:], mixed[:per]], 0))
        plain = jnp.concatenate(plain, 0).astype(jnp.bfloat16)
        turned = jnp.concatenate(turned, 0).astype(jnp.bfloat16)
        acc = jnp.dot(plain, beam[0], preferred_element_type=jnp.float32)
        acc = acc + jnp.dot(turned, beam[1], preferred_element_type=jnp.float32)
        for f in range(blocks):
            for r in range(per):
                first = f * wide + r * modes
                piece = acc[f * rows : (f + 1) * rows, first : first + modes]
                for c in range(2):
                    out[r, f, c : c + 1, :] = piece[c * per + r : c * per + r + 1]

    return pl.pallas_call(
        kernel,
        out_shape=jax.ShapeDtypeStruct((per, blocks, 2, modes), jnp.float32),
        in_specs=[pl.BlockSpec(memory_space=pltpu.VMEM)] * 6,
        out_specs=pl.BlockSpec(memory_space=pltpu.VMEM),
        compiler_params=pltpu.CompilerParams(vmem_limit_bytes=12 * MIB),
        name="couple",
    )(own, *others, spectra, turned_beams)


def shards(visibilities, beams, spectra, m_orders):
    size = lax.axis_size("wide")
    freqs = lax.axis_size("freq")
    pols = lax.axis_size("pol")
    per, blocks, _, modes, _ = beams.shape
    times = visibilities.shape[1]
    sums = transform(
        visibilities.transpose(0, 2, 3, 1).reshape(2, blocks * modes, times), m_orders, size
    )
    plan = PLAN if size == 4 else [[(w + s) % size for w in range(size)] for s in range(1, size)]
    own, *parts = cut(sums, plan)
    arrived = [own] + [
        lax.ppermute(part, ("wide", "pol"), pairs_of(step, pols)) for part, step in zip(parts, plan)
    ]
    total, partial = project(arrived, beams)

    def fetch(freq_step, pol_step):
        pairs = [
            (((f + freq_step) % freqs) * pols + (p + pol_step) % pols, f * pols + p)
            for f in range(freqs)
            for p in range(pols)
        ]
        return lax.ppermute(partial, ("freq", "pol"), pairs)

    cross, following, pol = fetch(1, 1), fetch(1, 0), fetch(0, 1)
    others = [cross, following, pol]
    msdata, turned = arrange(total, beams)
    return msdata, couple(partial, others, spectra, turned, modes)


def solution(mesh):
    return jax.shard_map(
        shards,
        mesh=mesh,
        in_specs=(
            P(None, ("grp", "wide"), "freq", "pol"),
            P("wide", "freq", None, "pol", None),
            P("freq", None, None),
            P(),
        ),
        out_specs=(
            P(("grp", "wide"), "freq", None, "pol"),
            P(("grp", "wide"), "freq", None, "pol"),
        ),
        check_vma=False,
    )
```

```python
import math

import jax
import jax.numpy as jnp
from jax import lax
from jax.experimental import pallas as pl
from jax.experimental.pallas import tpu as pltpu
from jax.sharding import PartitionSpec as P

TIME = 2048
BAND = 4
MIB = 1024 * 1024
PLAN = ((1, 3, 2, 0), (2, 1, 0, 3), (3, 0, 2, 1), (0, 2, 1, 3), (0, 1, 3, 2))


def tables(order, time):
    step = (order * time) & (TIME - 1)
    quarter = (step + TIME // 8) >> 9
    x = (step - (quarter << 9)).astype(jnp.float32) * (2.0 * math.pi / TIME)
    y = x * x
    sine = x * (1.0 + y * (-1.0 / 6 + y * (1.0 / 120 + y * (-1.0 / 5040 + y * (1.0 / 362880)))))
    cosine = 1.0 + y * (
        -0.5 + y * (1.0 / 24 + y * (-1.0 / 720 + y * (1.0 / 40320 + y * (-1.0 / 3628800))))
    )
    factor = 1.0 / math.sqrt(TIME)
    odd = (quarter & 1) == 1
    cos_sign = jnp.where(((quarter + 1) & 2) == 2, -factor, factor)
    sin_sign = jnp.where((quarter & 2) == 2, -factor, factor)
    return jnp.where(odd, sine, cosine) * cos_sign, jnp.where(odd, cosine, sine) * sin_sign


def split(value):
    high = value.astype(jnp.bfloat16)
    return high, (value - high.astype(jnp.float32)).astype(jnp.bfloat16)


def dot_last(left, right):
    return lax.dot_general(left, right, (((1,), (1,)), ((), ())), preferred_element_type=jnp.float32)


def pairs_of(step, pols):
    return [
        (w * pols + p, to * pols + (p if to != w else (p + 1) % pols))
        for w, to in enumerate(step)
        for p in range(pols)
    ]


def pin(array):
    return pltpu.with_memory_space_constraint(array, pltpu.HBM)


def transform(visibilities, m_orders, size):
    _, points, times = visibilities.shape
    total = m_orders.shape[0]
    per = total // size
    width = 256
    chunks = points // width

    def kernel(orders_ref, vis, *rest):
        out, held, orders, sems, order_sem = rest
        copies = [
            [
                pltpu.make_async_copy(
                    vis.at[c, pl.ds(n * width, width)], held.at[c, n], sems.at[c, n]
                )
                for c in range(2)
            ]
            for n in range(chunks)
        ]
        fetch = pltpu.make_async_copy(orders_ref, orders, order_sem)
        fetch.start()
        for pair in copies:
            for copy in pair:
                copy.start()
        fetch.wait()
        me = lax.axis_index("wide")
        row = lax.broadcasted_iota(jnp.int32, (total, times), 0)
        order = jnp.zeros((total, times), jnp.int32)
        for i in range(total):
            order = jnp.where(row == i, orders[i], order)
        time = lax.broadcasted_iota(jnp.int32, (total, times), 1) + me * times
        cosine, sine = tables(order, time)
        lefts = []
        for c in range(2):
            table = jnp.concatenate([cosine, -sine] if c == 0 else [sine, cosine], 0)
            high, low = split(table)
            lefts.append(jnp.concatenate([high, low], 0))
        sums = []
        for n in range(chunks):
            for copy in copies[n]:
                copy.wait()
            acc, small = None, None
            for c in range(2):
                high, low = split(held[c, n])
                rest = dot_last(low, lefts[c][: 2 * total])
                small = rest if small is None else small + rest
                both = dot_last(lefts[c], high)
                term = both[: 2 * total] + both[2 * total :]
                acc = term if acc is None else acc + term
            sums.append((acc, small))
        for n in range(chunks):
            acc = sums[n][0] + sums[n][1].T
            for s in range(size):
                for c in range(2):
                    first = c * total + s * per
                    out[s, c * per : (c + 1) * per, pl.ds(n * width, width)] = acc[first : first + per]

    return pl.pallas_call(
        kernel,
        out_shape=jax.ShapeDtypeStruct((size, 2 * per, points), jnp.float32),
        in_specs=[pl.BlockSpec(memory_space=pltpu.HBM)] * 2,
        out_specs=pl.BlockSpec(memory_space=pltpu.VMEM),
        scratch_shapes=[
            pltpu.VMEM((2, chunks, width, times), jnp.float32),
            pltpu.SMEM((total,), jnp.int32),
            pltpu.SemaphoreType.DMA((2, chunks)),
            pltpu.SemaphoreType.DMA,
        ],
        compiler_params=pltpu.CompilerParams(vmem_limit_bytes=12 * MIB),
        cost_estimate=pl.CostEstimate(
            flops=4 * 10**9, bytes_accessed=8 * 10**6, transcendentals=0
        ),
        name="transform",
    )(pin(m_orders), pin(visibilities))


def cut(sums, plan):
    size, rows, points = sums.shape

    def kernel(sums_ref, *outs):
        me = lax.axis_index("wide")
        outs[0][...] = sums_ref[me]
        for out, step in zip(outs[1:], plan):
            to = jnp.int32(step[0])
            for w in range(1, size):
                to = jnp.where(me == w, step[w], to)
            if any(step[w] == w for w in range(size)):
                out[...] = jnp.where(to == me, 0.0, sums_ref[to])
            else:
                out[...] = sums_ref[to]

    return pl.pallas_call(
        kernel,
        out_shape=[jax.ShapeDtypeStruct((rows, points), jnp.float32)] * (len(plan) + 1),
        in_specs=[pl.BlockSpec(memory_space=pltpu.VMEM)],
        out_specs=[pl.BlockSpec(memory_space=pltpu.VMEM)] * (len(plan) + 1),
        compiler_params=pltpu.CompilerParams(vmem_limit_bytes=4 * MIB),
        cost_estimate=pl.CostEstimate(flops=200 * 10**9, bytes_accessed=10**6, transcendentals=0),
        name="cut",
    )(sums)


def project(parts, beams):
    per, blocks, _, modes, degrees = beams.shape
    count = len(parts)

    def kernel(*refs):
        pieces, beam, total_out, proj_out = refs[:count], refs[count], refs[count + 1], refs[count + 2]
        row = lax.broadcasted_iota(jnp.int32, (2 * per, degrees), 0)
        total = pieces[0][...]
        for piece in pieces[1:]:
            total = total + piece[...]
        total_out[...] = total
        plain_all = total.astype(jnp.bfloat16)
        turned_all = jnp.concatenate([total[per:], -total[:per]], 0).astype(jnp.bfloat16)
        for f in range(blocks):
            plain = plain_all[:, f * modes : (f + 1) * modes]
            turned = turned_all[:, f * modes : (f + 1) * modes]
            acc = None
            for r in range(per):
                term = jnp.dot(plain, beam[r, f, 0], preferred_element_type=jnp.float32)
                term = term + jnp.dot(turned, beam[r, f, 1], preferred_element_type=jnp.float32)
                acc = term if acc is None else jnp.where(row % per == r, term, acc)
            proj_out[f] = acc

    return pl.pallas_call(
        kernel,
        out_shape=[
            jax.ShapeDtypeStruct((2 * per, blocks * modes), jnp.float32),
            jax.ShapeDtypeStruct((blocks, 2 * per, degrees), jnp.float32),
        ],
        in_specs=[pl.BlockSpec(memory_space=pltpu.VMEM)] * (count + 1),
        out_specs=[pl.BlockSpec(memory_space=pltpu.VMEM)] * 2,
        compiler_params=pltpu.CompilerParams(vmem_limit_bytes=12 * MIB),
        name="project",
    )(*parts, beams)


def arrange(total, per, blocks, modes):
    def kernel(total_ref, out):
        total_now = total_ref[...]
        for f in range(blocks):
            block = total_now[:, f * modes : (f + 1) * modes]
            for r in range(per):
                for c in range(2):
                    out[r, f, c : c + 1, :] = block[c * per + r : c * per + r + 1]

    return pl.pallas_call(
        kernel,
        out_shape=jax.ShapeDtypeStruct((per, blocks, 2, modes), jnp.float32),
        in_specs=[pl.BlockSpec(memory_space=pltpu.VMEM)],
        out_specs=pl.BlockSpec(memory_space=pltpu.VMEM),
        compiler_params=pltpu.CompilerParams(vmem_limit_bytes=4 * MIB),
        name="arrange",
    )(total)


def turn(beams):
    per, blocks, _, modes, degrees = beams.shape
    wide = per * modes

    def kernel(beam, turned):
        for f in range(blocks):
            for c in range(2):
                both = jnp.concatenate([beam[r, f, c] for r in range(per)], 0)
                turned[c, :, f * wide : (f + 1) * wide] = both.T

    return pl.pallas_call(
        kernel,
        out_shape=jax.ShapeDtypeStruct((2, degrees, blocks * wide), jnp.bfloat16),
        in_specs=[pl.BlockSpec(memory_space=pltpu.VMEM)],
        out_specs=pl.BlockSpec(memory_space=pltpu.VMEM),
        compiler_params=pltpu.CompilerParams(vmem_limit_bytes=16 * MIB),
        cost_estimate=pl.CostEstimate(flops=10**9, bytes_accessed=10**7, transcendentals=0),
        name="turn",
    )(beams)


def couple(own, others, spectra, turned_beams, modes):
    blocks, rows, degrees = own.shape
    per = rows // 2
    wide = per * modes

    def kernel(own_ref, cross_ref, next_ref, pol_ref, spec, beam, out):
        summed = [own_ref[f] + pol_ref[f] for f in range(blocks)]
        summed += [next_ref[f] + cross_ref[f] for f in range(blocks)]
        plain, turned = [], []
        for f in range(blocks):
            mixed = None
            for d in range(BAND + 1):
                term = spec[f, d : d + 1, :] * summed[f + d]
                mixed = term if mixed is None else mixed + term
            plain.append(mixed)
            turned.append(jnp.concatenate([-mixed[per:], mixed[:per]], 0))
        plain = jnp.concatenate(plain, 0).astype(jnp.bfloat16)
        turned = jnp.concatenate(turned, 0).astype(jnp.bfloat16)
        acc = jnp.dot(plain, beam[0], preferred_element_type=jnp.float32)
        acc = acc + jnp.dot(turned, beam[1], preferred_element_type=jnp.float32)
        for f in range(blocks):
            for r in range(per):
                first = f * wide + r * modes
                piece = acc[f * rows : (f + 1) * rows, first : first + modes]
                for c in range(2):
                    out[r, f, c : c + 1, :] = piece[c * per + r : c * per + r + 1]

    return pl.pallas_call(
        kernel,
        out_shape=jax.ShapeDtypeStruct((per, blocks, 2, modes), jnp.float32),
        in_specs=[pl.BlockSpec(memory_space=pltpu.VMEM)] * 6,
        out_specs=pl.BlockSpec(memory_space=pltpu.VMEM),
        compiler_params=pltpu.CompilerParams(vmem_limit_bytes=12 * MIB),
        name="couple",
    )(own, *others, spectra, turned_beams)


def shards(visibilities, beams, spectra, m_orders):
    size = lax.axis_size("wide")
    freqs = lax.axis_size("freq")
    pols = lax.axis_size("pol")
    per, blocks, _, modes, _ = beams.shape
    times = visibilities.shape[1]
    sums = transform(
        visibilities.transpose(0, 2, 3, 1).reshape(2, blocks * modes, times), m_orders, size
    )
    plan = PLAN if size == 4 else [[(w + s) % size for w in range(size)] for s in range(1, size)]
    own, *parts = cut(sums, plan)
    arrived = [own] + [
        lax.ppermute(part, ("wide", "pol"), pairs_of(step, pols)) for part, step in zip(parts, plan)
    ]
    total, partial = project(arrived, beams)

    def fetch(freq_step, pol_step):
        pairs = [
            (((f + freq_step) % freqs) * pols + (p + pol_step) % pols, f * pols + p)
            for f in range(freqs)
            for p in range(pols)
        ]
        return lax.ppermute(partial, ("freq", "pol"), pairs)

    cross, following, pol = fetch(1, 1), fetch(1, 0), fetch(0, 1)
    others = [cross, following, pol]
    msdata, turned = arrange(total, per, blocks, modes), turn(beams)
    return msdata, couple(partial, others, spectra, turned, modes)


def solution(mesh):
    return jax.shard_map(
        shards,
        mesh=mesh,
        in_specs=(
            P(None, ("grp", "wide"), "freq", "pol"),
            P("wide", "freq", None, "pol", None),
            P("freq", None, None),
            P(),
        ),
        out_specs=(
            P(("grp", "wide"), "freq", None, "pol"),
            P(("grp", "wide"), "freq", None, "pol"),
        ),
        check_vma=False,
    )
```

```python
import math

import jax
import jax.numpy as jnp
from jax import lax
from jax.experimental import pallas as pl
from jax.experimental.pallas import tpu as pltpu
from jax.sharding import PartitionSpec as P

TIME = 2048
BAND = 4
MIB = 1024 * 1024
PLAN = ((1, 3, 2, 0), (2, 1, 0, 3), (3, 0, 2, 1), (0, 2, 1, 3), (0, 1, 3, 2))


def tables(order, time):
    step = (order * time) & (TIME - 1)
    quarter = (step + TIME // 8) >> 9
    x = (step - (quarter << 9)).astype(jnp.float32) * (2.0 * math.pi / TIME)
    y = x * x
    sine = x * (1.0 + y * (-1.0 / 6 + y * (1.0 / 120 + y * (-1.0 / 5040 + y * (1.0 / 362880)))))
    cosine = 1.0 + y * (
        -0.5 + y * (1.0 / 24 + y * (-1.0 / 720 + y * (1.0 / 40320 + y * (-1.0 / 3628800))))
    )
    factor = 1.0 / math.sqrt(TIME)
    odd = (quarter & 1) == 1
    cos_sign = jnp.where(((quarter + 1) & 2) == 2, -factor, factor)
    sin_sign = jnp.where((quarter & 2) == 2, -factor, factor)
    return jnp.where(odd, sine, cosine) * cos_sign, jnp.where(odd, cosine, sine) * sin_sign


def split(value):
    high = value.astype(jnp.bfloat16)
    return high, (value - high.astype(jnp.float32)).astype(jnp.bfloat16)


def dot_last(left, right):
    return lax.dot_general(left, right, (((1,), (1,)), ((), ())), preferred_element_type=jnp.float32)


def pairs_of(step, pols):
    return [
        (w * pols + p, to * pols + (p if to != w else (p + 1) % pols))
        for w, to in enumerate(step)
        for p in range(pols)
    ]


def pin(array):
    return pltpu.with_memory_space_constraint(array, pltpu.HBM)


def transform(visibilities, m_orders, size):
    _, points, times = visibilities.shape
    total = m_orders.shape[0]
    per = total // size
    width = 256
    chunks = points // width

    def kernel(orders_ref, vis, *rest):
        out, held, orders, sems, order_sem = rest
        copies = [
            pltpu.make_async_copy(
                vis.at[:, pl.ds(n * width, width)], held.at[:, n], sems.at[n]
            )
            for n in range(chunks)
        ]
        fetch = pltpu.make_async_copy(orders_ref, orders, order_sem)
        fetch.start()
        for copy in copies:
            copy.start()
        fetch.wait()
        me = lax.axis_index("wide")
        row = lax.broadcasted_iota(jnp.int32, (total, times), 0)
        order = jnp.zeros((total, times), jnp.int32)
        for i in range(total):
            order = jnp.where(row == i, orders[i], order)
        time = lax.broadcasted_iota(jnp.int32, (total, times), 1) + me * times
        cosine, sine = tables(order, time)
        lefts = []
        for c in range(2):
            table = jnp.concatenate([cosine, -sine] if c == 0 else [sine, cosine], 0)
            high, low = split(table)
            lefts.append(jnp.concatenate([high, low], 0))
        sums = []
        for n in range(chunks):
            copies[n].wait()
            acc, small = None, None
            for c in range(2):
                high, low = split(held[c, n])
                rest = dot_last(low, lefts[c][: 2 * total])
                small = rest if small is None else small + rest
                both = dot_last(lefts[c], high)
                term = both[: 2 * total] + both[2 * total :]
                acc = term if acc is None else acc + term
            sums.append((acc, small))
        for n in range(chunks):
            acc = sums[n][0] + sums[n][1].T
            for s in range(size):
                for c in range(2):
                    first = c * total + s * per
                    out[s, c * per : (c + 1) * per, pl.ds(n * width, width)] = acc[first : first + per]

    return pl.pallas_call(
        kernel,
        out_shape=jax.ShapeDtypeStruct((size, 2 * per, points), jnp.float32),
        in_specs=[pl.BlockSpec(memory_space=pltpu.HBM)] * 2,
        out_specs=pl.BlockSpec(memory_space=pltpu.VMEM),
        scratch_shapes=[
            pltpu.VMEM((2, chunks, width, times), jnp.float32),
            pltpu.SMEM((total,), jnp.int32),
            pltpu.SemaphoreType.DMA((chunks,)),
            pltpu.SemaphoreType.DMA,
        ],
        compiler_params=pltpu.CompilerParams(vmem_limit_bytes=12 * MIB),
        cost_estimate=pl.CostEstimate(
            flops=4 * 10**9, bytes_accessed=8 * 10**6, transcendentals=0
        ),
        name="transform",
    )(pin(m_orders), pin(visibilities))


def cut(sums, plan):
    size, rows, points = sums.shape

    def kernel(sums_ref, *outs):
        me = lax.axis_index("wide")
        outs[0][...] = sums_ref[me]
        for out, step in zip(outs[1:], plan):
            to = jnp.int32(step[0])
            for w in range(1, size):
                to = jnp.where(me == w, step[w], to)
            if any(step[w] == w for w in range(size)):
                out[...] = jnp.where(to == me, 0.0, sums_ref[to])
            else:
                out[...] = sums_ref[to]

    return pl.pallas_call(
        kernel,
        out_shape=[jax.ShapeDtypeStruct((rows, points), jnp.float32)] * (len(plan) + 1),
        in_specs=[pl.BlockSpec(memory_space=pltpu.VMEM)],
        out_specs=[pl.BlockSpec(memory_space=pltpu.VMEM)] * (len(plan) + 1),
        compiler_params=pltpu.CompilerParams(vmem_limit_bytes=4 * MIB),
        cost_estimate=pl.CostEstimate(flops=200 * 10**9, bytes_accessed=10**6, transcendentals=0),
        name="cut",
    )(sums)


def project(parts, beams):
    per, blocks, _, modes, degrees = beams.shape
    count = len(parts)

    def kernel(*refs):
        pieces, beam, total_out, proj_out = refs[:count], refs[count], refs[count + 1], refs[count + 2]
        row = lax.broadcasted_iota(jnp.int32, (2 * per, degrees), 0)
        total = pieces[0][...]
        for piece in pieces[1:]:
            total = total + piece[...]
        total_out[...] = total
        plain_all = total.astype(jnp.bfloat16)
        turned_all = jnp.concatenate([total[per:], -total[:per]], 0).astype(jnp.bfloat16)
        for f in range(blocks):
            plain = plain_all[:, f * modes : (f + 1) * modes]
            turned = turned_all[:, f * modes : (f + 1) * modes]
            acc = None
            for r in range(per):
                term = jnp.dot(plain, beam[r, f, 0], preferred_element_type=jnp.float32)
                term = term + jnp.dot(turned, beam[r, f, 1], preferred_element_type=jnp.float32)
                acc = term if acc is None else jnp.where(row % per == r, term, acc)
            proj_out[f] = acc

    return pl.pallas_call(
        kernel,
        out_shape=[
            jax.ShapeDtypeStruct((2 * per, blocks * modes), jnp.float32),
            jax.ShapeDtypeStruct((blocks, 2 * per, degrees), jnp.float32),
        ],
        in_specs=[pl.BlockSpec(memory_space=pltpu.VMEM)] * (count + 1),
        out_specs=[pl.BlockSpec(memory_space=pltpu.VMEM)] * 2,
        compiler_params=pltpu.CompilerParams(vmem_limit_bytes=12 * MIB),
        name="project",
    )(*parts, beams)


def arrange(total, per, blocks, modes):
    def kernel(total_ref, out):
        total_now = total_ref[...]
        for f in range(blocks):
            block = total_now[:, f * modes : (f + 1) * modes]
            for r in range(per):
                for c in range(2):
                    out[r, f, c : c + 1, :] = block[c * per + r : c * per + r + 1]

    return pl.pallas_call(
        kernel,
        out_shape=jax.ShapeDtypeStruct((per, blocks, 2, modes), jnp.float32),
        in_specs=[pl.BlockSpec(memory_space=pltpu.VMEM)],
        out_specs=pl.BlockSpec(memory_space=pltpu.VMEM),
        compiler_params=pltpu.CompilerParams(vmem_limit_bytes=4 * MIB),
        name="arrange",
    )(total)


def turn(beams):
    per, blocks, _, modes, degrees = beams.shape
    wide = per * modes

    def kernel(beam, turned):
        for f in range(blocks):
            for c in range(2):
                both = jnp.concatenate([beam[r, f, c] for r in range(per)], 0)
                turned[c, :, f * wide : (f + 1) * wide] = both.T

    return pl.pallas_call(
        kernel,
        out_shape=jax.ShapeDtypeStruct((2, degrees, blocks * wide), jnp.bfloat16),
        in_specs=[pl.BlockSpec(memory_space=pltpu.VMEM)],
        out_specs=pl.BlockSpec(memory_space=pltpu.VMEM),
        compiler_params=pltpu.CompilerParams(vmem_limit_bytes=16 * MIB),
        cost_estimate=pl.CostEstimate(flops=10**9, bytes_accessed=10**7, transcendentals=0),
        name="turn",
    )(beams)


def couple(own, others, spectra, turned_beams, modes):
    blocks, rows, degrees = own.shape
    per = rows // 2
    wide = per * modes

    def kernel(own_ref, cross_ref, next_ref, pol_ref, spec, beam, out):
        summed = [own_ref[f] + pol_ref[f] for f in range(blocks)]
        summed += [next_ref[f] + cross_ref[f] for f in range(blocks)]
        plain, turned = [], []
        for f in range(blocks):
            mixed = None
            for d in range(BAND + 1):
                term = spec[f, d : d + 1, :] * summed[f + d]
                mixed = term if mixed is None else mixed + term
            plain.append(mixed)
            turned.append(jnp.concatenate([-mixed[per:], mixed[:per]], 0))
        plain = jnp.concatenate(plain, 0).astype(jnp.bfloat16)
        turned = jnp.concatenate(turned, 0).astype(jnp.bfloat16)
        acc = jnp.dot(plain, beam[0], preferred_element_type=jnp.float32)
        acc = acc + jnp.dot(turned, beam[1], preferred_element_type=jnp.float32)
        for f in range(blocks):
            for r in range(per):
                first = f * wide + r * modes
                piece = acc[f * rows : (f + 1) * rows, first : first + modes]
                for c in range(2):
                    out[r, f, c : c + 1, :] = piece[c * per + r : c * per + r + 1]

    return pl.pallas_call(
        kernel,
        out_shape=jax.ShapeDtypeStruct((per, blocks, 2, modes), jnp.float32),
        in_specs=[pl.BlockSpec(memory_space=pltpu.VMEM)] * 6,
        out_specs=pl.BlockSpec(memory_space=pltpu.VMEM),
        compiler_params=pltpu.CompilerParams(vmem_limit_bytes=12 * MIB),
        name="couple",
    )(own, *others, spectra, turned_beams)


def shards(visibilities, beams, spectra, m_orders):
    size = lax.axis_size("wide")
    freqs = lax.axis_size("freq")
    pols = lax.axis_size("pol")
    per, blocks, _, modes, _ = beams.shape
    times = visibilities.shape[1]
    sums = transform(
        visibilities.transpose(0, 2, 3, 1).reshape(2, blocks * modes, times), m_orders, size
    )
    plan = PLAN if size == 4 else [[(w + s) % size for w in range(size)] for s in range(1, size)]
    own, *parts = cut(sums, plan)
    arrived = [own] + [
        lax.ppermute(part, ("wide", "pol"), pairs_of(step, pols)) for part, step in zip(parts, plan)
    ]
    total, partial = project(arrived, beams)

    def fetch(freq_step, pol_step):
        pairs = [
            (((f + freq_step) % freqs) * pols + (p + pol_step) % pols, f * pols + p)
            for f in range(freqs)
            for p in range(pols)
        ]
        return lax.ppermute(partial, ("freq", "pol"), pairs)

    cross, following, pol = fetch(1, 1), fetch(1, 0), fetch(0, 1)
    others = [cross, following, pol]
    msdata, turned = arrange(total, per, blocks, modes), turn(beams)
    return msdata, couple(partial, others, spectra, turned, modes)


def solution(mesh):
    return jax.shard_map(
        shards,
        mesh=mesh,
        in_specs=(
            P(None, ("grp", "wide"), "freq", "pol"),
            P("wide", "freq", None, "pol", None),
            P("freq", None, None),
            P(),
        ),
        out_specs=(
            P(("grp", "wide"), "freq", None, "pol"),
            P(("grp", "wide"), "freq", None, "pol"),
        ),
        check_vma=False,
    )
```

```python
import math

import jax
import jax.numpy as jnp
from jax import lax
from jax.experimental import pallas as pl
from jax.experimental.pallas import tpu as pltpu
from jax.sharding import PartitionSpec as P

TIME = 2048
BAND = 4
MIB = 1024 * 1024
PLAN = ((1, 3, 2, 0), (2, 1, 0, 3), (3, 0, 2, 1), (0, 2, 1, 3), (0, 1, 3, 2))


def tables(order, time):
    step = (order * time) & (TIME - 1)
    quarter = (step + TIME // 8) >> 9
    x = (step - (quarter << 9)).astype(jnp.float32) * (2.0 * math.pi / TIME)
    y = x * x
    sine = x * (1.0 + y * (-1.0 / 6 + y * (1.0 / 120 + y * (-1.0 / 5040 + y * (1.0 / 362880)))))
    cosine = 1.0 + y * (
        -0.5 + y * (1.0 / 24 + y * (-1.0 / 720 + y * (1.0 / 40320 + y * (-1.0 / 3628800))))
    )
    factor = 1.0 / math.sqrt(TIME)
    odd = (quarter & 1) == 1
    cos_sign = jnp.where(((quarter + 1) & 2) == 2, -factor, factor)
    sin_sign = jnp.where((quarter & 2) == 2, -factor, factor)
    return jnp.where(odd, sine, cosine) * cos_sign, jnp.where(odd, cosine, sine) * sin_sign


def split(value):
    high = value.astype(jnp.bfloat16)
    return high, (value - high.astype(jnp.float32)).astype(jnp.bfloat16)


def dot_last(left, right):
    return lax.dot_general(left, right, (((1,), (1,)), ((), ())), preferred_element_type=jnp.float32)


def pairs_of(step, pols):
    return [
        (w * pols + p, to * pols + (p if to != w else (p + 1) % pols))
        for w, to in enumerate(step)
        for p in range(pols)
    ]


def pin(array):
    return pltpu.with_memory_space_constraint(array, pltpu.HBM)


def transform(visibilities, m_orders, size):
    _, points, times = visibilities.shape
    total = m_orders.shape[0]
    per = total // size
    width = 256
    chunks = points // width

    def kernel(orders_ref, vis, *rest):
        out, held, orders, sems, order_sem = rest
        copies = [
            [
                pltpu.make_async_copy(
                    vis.at[c, pl.ds(n * width, width)], held.at[c, n], sems.at[c, n]
                )
                for c in range(2)
            ]
            for n in range(chunks)
        ]
        fetch = pltpu.make_async_copy(orders_ref, orders, order_sem)
        for copy in copies[0]:
            copy.start()
        fetch.start()
        for pair in copies[1:]:
            for copy in pair:
                copy.start()
        fetch.wait()
        me = lax.axis_index("wide")
        row = lax.broadcasted_iota(jnp.int32, (total, times), 0)
        order = jnp.zeros((total, times), jnp.int32)
        for i in range(total):
            order = jnp.where(row == i, orders[i], order)
        time = lax.broadcasted_iota(jnp.int32, (total, times), 1) + me * times
        cosine, sine = tables(order, time)
        lefts = []
        for c in range(2):
            table = jnp.concatenate([cosine, -sine] if c == 0 else [sine, cosine], 0)
            high, low = split(table)
            lefts.append(jnp.concatenate([high, low], 0))
        sums = []
        for n in range(chunks):
            for copy in copies[n]:
                copy.wait()
            acc, small = None, None
            for c in range(2):
                high, low = split(held[c, n])
                rest = dot_last(low, lefts[c][: 2 * total])
                small = rest if small is None else small + rest
                both = dot_last(lefts[c], high)
                term = both[: 2 * total] + both[2 * total :]
                acc = term if acc is None else acc + term
            sums.append((acc, small))
        for n in range(chunks):
            acc = sums[n][0] + sums[n][1].T
            for s in range(size):
                for c in range(2):
                    first = c * total + s * per
                    out[s, c * per : (c + 1) * per, pl.ds(n * width, width)] = acc[first : first + per]

    return pl.pallas_call(
        kernel,
        out_shape=jax.ShapeDtypeStruct((size, 2 * per, points), jnp.float32),
        in_specs=[pl.BlockSpec(memory_space=pltpu.HBM)] * 2,
        out_specs=pl.BlockSpec(memory_space=pltpu.VMEM),
        scratch_shapes=[
            pltpu.VMEM((2, chunks, width, times), jnp.float32),
            pltpu.SMEM((total,), jnp.int32),
            pltpu.SemaphoreType.DMA((2, chunks)),
            pltpu.SemaphoreType.DMA,
        ],
        compiler_params=pltpu.CompilerParams(vmem_limit_bytes=12 * MIB),
        cost_estimate=pl.CostEstimate(
            flops=4 * 10**9, bytes_accessed=8 * 10**6, transcendentals=0
        ),
        name="transform",
    )(pin(m_orders), pin(visibilities))


def cut(sums, plan):
    size, rows, points = sums.shape

    def kernel(sums_ref, *outs):
        me = lax.axis_index("wide")
        outs[0][...] = sums_ref[me]
        for out, step in zip(outs[1:], plan):
            to = jnp.int32(step[0])
            for w in range(1, size):
                to = jnp.where(me == w, step[w], to)
            if any(step[w] == w for w in range(size)):
                out[...] = jnp.where(to == me, 0.0, sums_ref[to])
            else:
                out[...] = sums_ref[to]

    return pl.pallas_call(
        kernel,
        out_shape=[jax.ShapeDtypeStruct((rows, points), jnp.float32)] * (len(plan) + 1),
        in_specs=[pl.BlockSpec(memory_space=pltpu.VMEM)],
        out_specs=[pl.BlockSpec(memory_space=pltpu.VMEM)] * (len(plan) + 1),
        compiler_params=pltpu.CompilerParams(vmem_limit_bytes=4 * MIB),
        cost_estimate=pl.CostEstimate(flops=200 * 10**9, bytes_accessed=10**6, transcendentals=0),
        name="cut",
    )(sums)


def project(parts, beams):
    per, blocks, _, modes, degrees = beams.shape
    count = len(parts)

    def kernel(*refs):
        pieces, beam, total_out, proj_out = refs[:count], refs[count], refs[count + 1], refs[count + 2]
        row = lax.broadcasted_iota(jnp.int32, (2 * per, degrees), 0)
        total = pieces[0][...]
        for piece in pieces[1:]:
            total = total + piece[...]
        total_out[...] = total
        plain_all = total.astype(jnp.bfloat16)
        turned_all = jnp.concatenate([total[per:], -total[:per]], 0).astype(jnp.bfloat16)
        for f in range(blocks):
            plain = plain_all[:, f * modes : (f + 1) * modes]
            turned = turned_all[:, f * modes : (f + 1) * modes]
            acc = None
            for r in range(per):
                term = jnp.dot(plain, beam[r, f, 0], preferred_element_type=jnp.float32)
                term = term + jnp.dot(turned, beam[r, f, 1], preferred_element_type=jnp.float32)
                acc = term if acc is None else jnp.where(row % per == r, term, acc)
            proj_out[f] = acc

    return pl.pallas_call(
        kernel,
        out_shape=[
            jax.ShapeDtypeStruct((2 * per, blocks * modes), jnp.float32),
            jax.ShapeDtypeStruct((blocks, 2 * per, degrees), jnp.float32),
        ],
        in_specs=[pl.BlockSpec(memory_space=pltpu.VMEM)] * (count + 1),
        out_specs=[pl.BlockSpec(memory_space=pltpu.VMEM)] * 2,
        compiler_params=pltpu.CompilerParams(vmem_limit_bytes=12 * MIB),
        name="project",
    )(*parts, beams)


def arrange(total, per, blocks, modes):
    def kernel(total_ref, out):
        total_now = total_ref[...]
        for f in range(blocks):
            block = total_now[:, f * modes : (f + 1) * modes]
            for r in range(per):
                for c in range(2):
                    out[r, f, c : c + 1, :] = block[c * per + r : c * per + r + 1]

    return pl.pallas_call(
        kernel,
        out_shape=jax.ShapeDtypeStruct((per, blocks, 2, modes), jnp.float32),
        in_specs=[pl.BlockSpec(memory_space=pltpu.VMEM)],
        out_specs=pl.BlockSpec(memory_space=pltpu.VMEM),
        compiler_params=pltpu.CompilerParams(vmem_limit_bytes=4 * MIB),
        name="arrange",
    )(total)


def turn(beams):
    per, blocks, _, modes, degrees = beams.shape
    wide = per * modes

    def kernel(beam, turned):
        for f in range(blocks):
            for c in range(2):
                both = jnp.concatenate([beam[r, f, c] for r in range(per)], 0)
                turned[c, :, f * wide : (f + 1) * wide] = both.T

    return pl.pallas_call(
        kernel,
        out_shape=jax.ShapeDtypeStruct((2, degrees, blocks * wide), jnp.bfloat16),
        in_specs=[pl.BlockSpec(memory_space=pltpu.VMEM)],
        out_specs=pl.BlockSpec(memory_space=pltpu.VMEM),
        compiler_params=pltpu.CompilerParams(vmem_limit_bytes=16 * MIB),
        cost_estimate=pl.CostEstimate(flops=10**9, bytes_accessed=10**7, transcendentals=0),
        name="turn",
    )(beams)


def couple(own, others, spectra, turned_beams, modes):
    blocks, rows, degrees = own.shape
    per = rows // 2
    wide = per * modes

    def kernel(own_ref, cross_ref, next_ref, pol_ref, spec, beam, out):
        summed = [own_ref[f] + pol_ref[f] for f in range(blocks)]
        summed += [next_ref[f] + cross_ref[f] for f in range(blocks)]
        plain, turned = [], []
        for f in range(blocks):
            mixed = None
            for d in range(BAND + 1):
                term = spec[f, d : d + 1, :] * summed[f + d]
                mixed = term if mixed is None else mixed + term
            plain.append(mixed)
            turned.append(jnp.concatenate([-mixed[per:], mixed[:per]], 0))
        plain = jnp.concatenate(plain, 0).astype(jnp.bfloat16)
        turned = jnp.concatenate(turned, 0).astype(jnp.bfloat16)
        acc = jnp.dot(plain, beam[0], preferred_element_type=jnp.float32)
        acc = acc + jnp.dot(turned, beam[1], preferred_element_type=jnp.float32)
        for f in range(blocks):
            for r in range(per):
                first = f * wide + r * modes
                piece = acc[f * rows : (f + 1) * rows, first : first + modes]
                for c in range(2):
                    out[r, f, c : c + 1, :] = piece[c * per + r : c * per + r + 1]

    return pl.pallas_call(
        kernel,
        out_shape=jax.ShapeDtypeStruct((per, blocks, 2, modes), jnp.float32),
        in_specs=[pl.BlockSpec(memory_space=pltpu.VMEM)] * 6,
        out_specs=pl.BlockSpec(memory_space=pltpu.VMEM),
        compiler_params=pltpu.CompilerParams(vmem_limit_bytes=12 * MIB),
        name="couple",
    )(own, *others, spectra, turned_beams)


def shards(visibilities, beams, spectra, m_orders):
    size = lax.axis_size("wide")
    freqs = lax.axis_size("freq")
    pols = lax.axis_size("pol")
    per, blocks, _, modes, _ = beams.shape
    times = visibilities.shape[1]
    sums = transform(
        visibilities.transpose(0, 2, 3, 1).reshape(2, blocks * modes, times), m_orders, size
    )
    plan = PLAN if size == 4 else [[(w + s) % size for w in range(size)] for s in range(1, size)]
    own, *parts = cut(sums, plan)
    arrived = [own] + [
        lax.ppermute(part, ("wide", "pol"), pairs_of(step, pols)) for part, step in zip(parts, plan)
    ]
    total, partial = project(arrived, beams)

    def fetch(freq_step, pol_step):
        pairs = [
            (((f + freq_step) % freqs) * pols + (p + pol_step) % pols, f * pols + p)
            for f in range(freqs)
            for p in range(pols)
        ]
        return lax.ppermute(partial, ("freq", "pol"), pairs)

    cross, following, pol = fetch(1, 1), fetch(1, 0), fetch(0, 1)
    others = [cross, following, pol]
    msdata, turned = arrange(total, per, blocks, modes), turn(beams)
    return msdata, couple(partial, others, spectra, turned, modes)


def solution(mesh):
    return jax.shard_map(
        shards,
        mesh=mesh,
        in_specs=(
            P(None, ("grp", "wide"), "freq", "pol"),
            P("wide", "freq", None, "pol", None),
            P("freq", None, None),
            P(),
        ),
        out_specs=(
            P(("grp", "wide"), "freq", None, "pol"),
            P(("grp", "wide"), "freq", None, "pol"),
        ),
        check_vma=False,
    )
```

```python
import math

import jax
import jax.numpy as jnp
from jax import lax
from jax.experimental import pallas as pl
from jax.experimental.pallas import tpu as pltpu
from jax.sharding import PartitionSpec as P

TIME = 2048
BAND = 4
MIB = 1024 * 1024
PLAN = ((1, 3, 2, 0), (2, 1, 0, 3), (3, 0, 2, 1), (0, 2, 1, 3), (0, 1, 3, 2))


def tables(order, time):
    step = (order * time) & (TIME - 1)
    quarter = (step + TIME // 8) >> 9
    x = (step - (quarter << 9)).astype(jnp.float32) * (2.0 * math.pi / TIME)
    y = x * x
    sine = x * (1.0 + y * (-1.0 / 6 + y * (1.0 / 120 + y * (-1.0 / 5040 + y * (1.0 / 362880)))))
    cosine = 1.0 + y * (
        -0.5 + y * (1.0 / 24 + y * (-1.0 / 720 + y * (1.0 / 40320 + y * (-1.0 / 3628800))))
    )
    factor = 1.0 / math.sqrt(TIME)
    odd = (quarter & 1) == 1
    cos_sign = jnp.where(((quarter + 1) & 2) == 2, -factor, factor)
    sin_sign = jnp.where((quarter & 2) == 2, -factor, factor)
    return jnp.where(odd, sine, cosine) * cos_sign, jnp.where(odd, cosine, sine) * sin_sign


def split(value):
    high = value.astype(jnp.bfloat16)
    return high, (value - high.astype(jnp.float32)).astype(jnp.bfloat16)


def dot_last(left, right):
    return lax.dot_general(left, right, (((1,), (1,)), ((), ())), preferred_element_type=jnp.float32)


def pairs_of(step, pols):
    return [
        (w * pols + p, to * pols + (p if to != w else (p + 1) % pols))
        for w, to in enumerate(step)
        for p in range(pols)
    ]


def pin(array):
    return pltpu.with_memory_space_constraint(array, pltpu.HBM)


def transform(visibilities, m_orders, size):
    _, points, times = visibilities.shape
    total = m_orders.shape[0]
    per = total // size
    width = 256
    chunks = points // width

    def kernel(orders_ref, vis, *rest):
        out, held, orders, sems, order_sem = rest
        copies = [
            [
                pltpu.make_async_copy(
                    vis.at[c, pl.ds(n * width, width)], held.at[c, n], sems.at[c, n]
                )
                for c in range(2)
            ]
            for n in range(chunks)
        ]
        fetch = pltpu.make_async_copy(orders_ref, orders, order_sem)
        fetch.start()
        for pair in copies:
            for copy in pair:
                copy.start()
        fetch.wait()
        me = lax.axis_index("wide")
        row = lax.broadcasted_iota(jnp.int32, (total, times), 0)
        order = jnp.zeros((total, times), jnp.int32)
        for i in range(total):
            order = jnp.where(row == i, orders[i], order)
        time = lax.broadcasted_iota(jnp.int32, (total, times), 1) + me * times
        cosine, sine = tables(order, time)
        lefts = []
        for c in range(2):
            table = jnp.concatenate([cosine, -sine] if c == 0 else [sine, cosine], 0)
            high, low = split(table)
            lefts.append(jnp.concatenate([high, low], 0))
        sums = []
        for n in range(chunks):
            for copy in copies[n]:
                copy.wait()
            acc, small = None, None
            for c in range(2):
                high, low = split(held[c, n])
                rest = dot_last(low, lefts[c][: 2 * total])
                small = rest if small is None else small + rest
                both = dot_last(lefts[c], high)
                term = both[: 2 * total] + both[2 * total :]
                acc = term if acc is None else acc + term
            sums.append((acc, small))
            for m in [n - 1] * (n > 0) + [n] * (n == chunks - 1):
                acc = sums[m][0] + sums[m][1].T
                for s in range(size):
                    for c in range(2):
                        first = c * total + s * per
                        out[s, c * per : (c + 1) * per, pl.ds(m * width, width)] = acc[first : first + per]

    return pl.pallas_call(
        kernel,
        out_shape=jax.ShapeDtypeStruct((size, 2 * per, points), jnp.float32),
        in_specs=[pl.BlockSpec(memory_space=pltpu.HBM)] * 2,
        out_specs=pl.BlockSpec(memory_space=pltpu.VMEM),
        scratch_shapes=[
            pltpu.VMEM((2, chunks, width, times), jnp.float32),
            pltpu.SMEM((total,), jnp.int32),
            pltpu.SemaphoreType.DMA((2, chunks)),
            pltpu.SemaphoreType.DMA,
        ],
        compiler_params=pltpu.CompilerParams(vmem_limit_bytes=12 * MIB),
        cost_estimate=pl.CostEstimate(
            flops=4 * 10**9, bytes_accessed=8 * 10**6, transcendentals=0
        ),
        name="transform",
    )(pin(m_orders), pin(visibilities))


def cut(sums, plan):
    size, rows, points = sums.shape

    def kernel(sums_ref, *outs):
        me = lax.axis_index("wide")
        outs[0][...] = sums_ref[me]
        for out, step in zip(outs[1:], plan):
            to = jnp.int32(step[0])
            for w in range(1, size):
                to = jnp.where(me == w, step[w], to)
            if any(step[w] == w for w in range(size)):
                out[...] = jnp.where(to == me, 0.0, sums_ref[to])
            else:
                out[...] = sums_ref[to]

    return pl.pallas_call(
        kernel,
        out_shape=[jax.ShapeDtypeStruct((rows, points), jnp.float32)] * (len(plan) + 1),
        in_specs=[pl.BlockSpec(memory_space=pltpu.VMEM)],
        out_specs=[pl.BlockSpec(memory_space=pltpu.VMEM)] * (len(plan) + 1),
        compiler_params=pltpu.CompilerParams(vmem_limit_bytes=4 * MIB),
        cost_estimate=pl.CostEstimate(flops=200 * 10**9, bytes_accessed=10**6, transcendentals=0),
        name="cut",
    )(sums)


def project(parts, beams):
    per, blocks, _, modes, degrees = beams.shape
    count = len(parts)

    def kernel(*refs):
        pieces, beam, total_out, proj_out = refs[:count], refs[count], refs[count + 1], refs[count + 2]
        row = lax.broadcasted_iota(jnp.int32, (2 * per, degrees), 0)
        total = pieces[0][...]
        for piece in pieces[1:]:
            total = total + piece[...]
        total_out[...] = total
        plain_all = total.astype(jnp.bfloat16)
        turned_all = jnp.concatenate([total[per:], -total[:per]], 0).astype(jnp.bfloat16)
        for f in range(blocks):
            plain = plain_all[:, f * modes : (f + 1) * modes]
            turned = turned_all[:, f * modes : (f + 1) * modes]
            acc = None
            for r in range(per):
                term = jnp.dot(plain, beam[r, f, 0], preferred_element_type=jnp.float32)
                term = term + jnp.dot(turned, beam[r, f, 1], preferred_element_type=jnp.float32)
                acc = term if acc is None else jnp.where(row % per == r, term, acc)
            proj_out[f] = acc

    return pl.pallas_call(
        kernel,
        out_shape=[
            jax.ShapeDtypeStruct((2 * per, blocks * modes), jnp.float32),
            jax.ShapeDtypeStruct((blocks, 2 * per, degrees), jnp.float32),
        ],
        in_specs=[pl.BlockSpec(memory_space=pltpu.VMEM)] * (count + 1),
        out_specs=[pl.BlockSpec(memory_space=pltpu.VMEM)] * 2,
        compiler_params=pltpu.CompilerParams(vmem_limit_bytes=12 * MIB),
        name="project",
    )(*parts, beams)


def arrange(total, per, blocks, modes):
    def kernel(total_ref, out):
        total_now = total_ref[...]
        for f in range(blocks):
            block = total_now[:, f * modes : (f + 1) * modes]
            for r in range(per):
                for c in range(2):
                    out[r, f, c : c + 1, :] = block[c * per + r : c * per + r + 1]

    return pl.pallas_call(
        kernel,
        out_shape=jax.ShapeDtypeStruct((per, blocks, 2, modes), jnp.float32),
        in_specs=[pl.BlockSpec(memory_space=pltpu.VMEM)],
        out_specs=pl.BlockSpec(memory_space=pltpu.VMEM),
        compiler_params=pltpu.CompilerParams(vmem_limit_bytes=4 * MIB),
        name="arrange",
    )(total)


def turn(beams):
    per, blocks, _, modes, degrees = beams.shape
    wide = per * modes

    def kernel(beam, turned):
        for f in range(blocks):
            for c in range(2):
                both = jnp.concatenate([beam[r, f, c] for r in range(per)], 0)
                turned[c, :, f * wide : (f + 1) * wide] = both.T

    return pl.pallas_call(
        kernel,
        out_shape=jax.ShapeDtypeStruct((2, degrees, blocks * wide), jnp.bfloat16),
        in_specs=[pl.BlockSpec(memory_space=pltpu.VMEM)],
        out_specs=pl.BlockSpec(memory_space=pltpu.VMEM),
        compiler_params=pltpu.CompilerParams(vmem_limit_bytes=16 * MIB),
        cost_estimate=pl.CostEstimate(flops=10**9, bytes_accessed=10**7, transcendentals=0),
        name="turn",
    )(beams)


def couple(own, others, spectra, turned_beams, modes):
    blocks, rows, degrees = own.shape
    per = rows // 2
    wide = per * modes

    def kernel(own_ref, cross_ref, next_ref, pol_ref, spec, beam, out):
        summed = [own_ref[f] + pol_ref[f] for f in range(blocks)]
        summed += [next_ref[f] + cross_ref[f] for f in range(blocks)]
        plain, turned = [], []
        for f in range(blocks):
            mixed = None
            for d in range(BAND + 1):
                term = spec[f, d : d + 1, :] * summed[f + d]
                mixed = term if mixed is None else mixed + term
            plain.append(mixed)
            turned.append(jnp.concatenate([-mixed[per:], mixed[:per]], 0))
        plain = jnp.concatenate(plain, 0).astype(jnp.bfloat16)
        turned = jnp.concatenate(turned, 0).astype(jnp.bfloat16)
        acc = jnp.dot(plain, beam[0], preferred_element_type=jnp.float32)
        acc = acc + jnp.dot(turned, beam[1], preferred_element_type=jnp.float32)
        for f in range(blocks):
            for r in range(per):
                first = f * wide + r * modes
                piece = acc[f * rows : (f + 1) * rows, first : first + modes]
                for c in range(2):
                    out[r, f, c : c + 1, :] = piece[c * per + r : c * per + r + 1]

    return pl.pallas_call(
        kernel,
        out_shape=jax.ShapeDtypeStruct((per, blocks, 2, modes), jnp.float32),
        in_specs=[pl.BlockSpec(memory_space=pltpu.VMEM)] * 6,
        out_specs=pl.BlockSpec(memory_space=pltpu.VMEM),
        compiler_params=pltpu.CompilerParams(vmem_limit_bytes=12 * MIB),
        name="couple",
    )(own, *others, spectra, turned_beams)


def shards(visibilities, beams, spectra, m_orders):
    size = lax.axis_size("wide")
    freqs = lax.axis_size("freq")
    pols = lax.axis_size("pol")
    per, blocks, _, modes, _ = beams.shape
    times = visibilities.shape[1]
    sums = transform(
        visibilities.transpose(0, 2, 3, 1).reshape(2, blocks * modes, times), m_orders, size
    )
    plan = PLAN if size == 4 else [[(w + s) % size for w in range(size)] for s in range(1, size)]
    own, *parts = cut(sums, plan)
    arrived = [own] + [
        lax.ppermute(part, ("wide", "pol"), pairs_of(step, pols)) for part, step in zip(parts, plan)
    ]
    total, partial = project(arrived, beams)

    def fetch(freq_step, pol_step):
        pairs = [
            (((f + freq_step) % freqs) * pols + (p + pol_step) % pols, f * pols + p)
            for f in range(freqs)
            for p in range(pols)
        ]
        return lax.ppermute(partial, ("freq", "pol"), pairs)

    cross, following, pol = fetch(1, 1), fetch(1, 0), fetch(0, 1)
    others = [cross, following, pol]
    msdata, turned = arrange(total, per, blocks, modes), turn(beams)
    return msdata, couple(partial, others, spectra, turned, modes)


def solution(mesh):
    return jax.shard_map(
        shards,
        mesh=mesh,
        in_specs=(
            P(None, ("grp", "wide"), "freq", "pol"),
            P("wide", "freq", None, "pol", None),
            P("freq", None, None),
            P(),
        ),
        out_specs=(
            P(("grp", "wide"), "freq", None, "pol"),
            P(("grp", "wide"), "freq", None, "pol"),
        ),
        check_vma=False,
    )
```
